32 devices in a mesh: dp: 2 (over y), fsdp: 8 (over z, core), tensor: 2 (over x).
Axes of the slice: x: 2, y: 2, z: 4, core: 2. Of those that a mesh axis runs over, the one named last changes fastest.
Arguments:
- attn_out: bfloat16 [2048, 2560], P(('dp', 'fsdp')), may hold values from -6 to 6
- cotangent: bfloat16 [2048, 5120], P(('dp', 'fsdp'), 'tensor'), may hold values from -6 to 6
- old_weights: bfloat16 [3, 2048, 4096], P(None, 'tensor', 'fsdp'), may hold values from -0.125 to 0.125
- depth_coef: float32 [2], replicated, may hold values from 0.3 to 1
- depth_pick: int32 [2], replicated, may hold values from 0 to 2
- in_blocks: bfloat16 [20, 2, 128, 128], replicated, may hold values from -0.3125 to 0.3125
- in_cols: int32 [20, 2], replicated, may hold values from 0 to 15, all different within a row
- out_blocks: bfloat16 [40, 2, 128, 128], P('tensor'), may hold values from -0.375 to 0.375
- out_cols: int32 [40, 2], P('tensor'), may hold values from 0 to 31, all different within a row
Outputs:
- grown_out: bfloat16 [2048, 5120], P(('dp', 'fsdp'), 'tensor')
- grad_attn: bfloat16 [2048, 2560], P(('dp', 'fsdp'), 'tensor')
- grad_in_blocks: float32 [20, 2, 128, 128], P('tensor')
- grad_out_blocks: float32 [40, 2, 128, 128], P('tensor')
The draws below stay inside these ranges and needn't reach their ends.
Inputs may be any that keep to these rules, and one draw needn't show every extreme that they name: `in_cols`: each row names 2 different old head blocks; every old head block is named by some row. `out_cols`: each row names 2 different old width blocks; every old width block is named by some row.
All inputs are finite; a program needn't handle non-finite values.
Results may differ from the reference program's by a relative error of at most 0.0095.
Values may be sent and summed in bfloat16 or wider, within the bound.
A program may use at most 64 MiB of HBM per device.

```python
import jax
import jax.numpy as jnp
from jax import lax

HEAD = 128
D_OLD = 4096
D_NEW = 5120
HG_OLD = 16
HG_NEW = 20
L_OLD = 3
DEPTH_K = 2
K_IN = 2
K_OUT = 2
TOK_DEV = 128
TOKENS = 2048
F_OLD = 2048
F_NEW = 2560
BO_OLD = 32
BO_NEW = 40
N_TENSOR = 2


def level_of(key, extent, shards, low, largest):
    factor_of, own = 1.0, jax.random.fold_in(key, 6)
    for dim, blocks in shards:
        draws = jnp.exp(jax.random.uniform(jax.random.fold_in(own, dim), (blocks,), jnp.float32, low / len(shards), largest / len(shards)))
        factor_of = factor_of * jnp.repeat(draws, extent[dim] // blocks).reshape([-1 if axis == dim else 1 for axis in range(len(extent))])
    return factor_of


def different_ones(stream_key, rows, count, top, lift):
    ranking = jax.random.permutation(jax.random.fold_in(stream_key, 1), count)
    pull = ranking
    for power in range(3):
        pull = pull * pull // count
    pull = pull * lift // count
    lots = jax.random.randint(jax.random.fold_in(stream_key, 2), (rows, count), 0, 4096) + pull
    fixed_rows = jax.random.permutation(jax.random.fold_in(stream_key, 3), rows)[jnp.arange(count) % rows]
    lots = jnp.where(jnp.arange(rows)[:, None] == fixed_rows[None, :], 1 << 14, lots)
    priority = lots * count + jnp.arange(count)
    return lax.top_k(priority.astype(jnp.int32), top)[1].astype(jnp.int32)


def bell_draw(key, dims, width, reach, shards=(), kind=jnp.bfloat16):
    values = jax.random.normal(key, dims, jnp.float32) * width
    if len(shards) > 0:
        values = level_of(key, dims, shards, -0.22, 0.18) * values
    return jnp.clip(values, min=-reach, max=reach).astype(kind)


def setup_inputs(seed: int = 0) -> dict:
    streams_of = jax.random.split(jax.random.key(seed), 10)
    return {
        "attn_out": bell_draw(streams_of[0], (TOKENS, F_NEW), 1.0, 6.0, ((0, 16),)),
        "cotangent": bell_draw(streams_of[1], (TOKENS, D_NEW), 1.0, 6.0, ((0, 16), (1, 2))),
        "old_weights": bell_draw(streams_of[2], (L_OLD, F_OLD, D_OLD), F_OLD ** -0.5, 0.125, ((1, 2), (2, 8))),
        "depth_coef": jnp.clip(jax.random.uniform(streams_of[3], (DEPTH_K,), jnp.float32, 0.3, 1.0), 0.3, 1.0),
        "depth_pick": jax.random.randint(streams_of[4], (DEPTH_K,), 0, L_OLD).astype(jnp.int32),
        "in_blocks": bell_draw(streams_of[5], (HG_NEW, K_IN, HEAD, HEAD), (HEAD * K_IN * HG_NEW // HG_OLD) ** -0.5, 0.3125),
        "in_cols": different_ones(streams_of[6], HG_NEW, HG_OLD, K_IN, 0),
        "out_blocks": bell_draw(streams_of[7], (BO_NEW, K_OUT, HEAD, HEAD), (HEAD * K_OUT) ** -0.5, 0.375, ((0, 2),)),
        "out_cols": different_ones(streams_of[8], BO_NEW, BO_OLD, K_OUT, 0),
    }


def reference(attn_out, cotangent, old_weights, depth_coef, depth_pick, in_blocks, in_cols, out_blocks, out_cols):
    highest = lax.Precision.HIGHEST
    mixed_weight = jnp.zeros((F_OLD, D_OLD), jnp.float32)
    for layer_slot in range(DEPTH_K):
        picked = lax.dynamic_index_in_dim(old_weights, depth_pick[layer_slot], 0, keepdims=False)
        mixed_weight = mixed_weight + depth_coef[layer_slot] * picked.astype(jnp.float32)
    mixed_weight = mixed_weight.astype(jnp.bfloat16)
    mix_halves = mixed_weight.astype(jnp.float32).reshape(N_TENSOR, F_OLD // N_TENSOR, D_OLD)
    in_hot = (in_cols[:, :, None] == jnp.arange(HG_OLD, dtype=jnp.int32)[None, None, :]).astype(jnp.float32)
    out_hot = (out_cols[:, :, None] == jnp.arange(BO_OLD, dtype=jnp.int32)[None, None, :]).astype(jnp.float32)
    out_hot_halves = out_hot.reshape(N_TENSOR, BO_NEW // N_TENSOR, K_OUT, BO_OLD)
    in_weights = in_blocks.astype(jnp.float32)
    out_weights = out_blocks.astype(jnp.float32)
    out_halves = out_weights.reshape(N_TENSOR, BO_NEW // N_TENSOR, K_OUT, HEAD, HEAD)

    def token_block(totals, pieces):
        attn_rows, cot_rows = pieces
        attn_three = attn_rows.reshape(-1, HG_NEW, HEAD).astype(jnp.float32)
        products = jnp.einsum('trd,rkde->trke', attn_three, in_weights, precision=highest)
        hidden = jnp.einsum('trke,rkc->tce', products, in_hot, precision=highest).reshape(-1, F_OLD).astype(jnp.bfloat16)
        hidden_halves = hidden.astype(jnp.float32).reshape(-1, N_TENSOR, F_OLD // N_TENSOR)
        partials = jnp.einsum('tsf,sfo->tso', hidden_halves, mix_halves, precision=highest).astype(jnp.bfloat16)
        partials = lax.optimization_barrier(partials)
        old_out = jnp.sum(partials.astype(jnp.float32), axis=1).astype(jnp.bfloat16)
        old_selected = jnp.take(old_out.reshape(-1, BO_OLD, HEAD), out_cols, axis=1).astype(jnp.float32)
        grown = jnp.einsum('trkd,rkde->tre', old_selected, out_weights, precision=highest).reshape(-1, D_NEW).astype(jnp.bfloat16)
        cot_four = cot_rows.reshape(-1, N_TENSOR, BO_NEW // N_TENSOR, HEAD).astype(jnp.float32)
        backward_terms = jnp.einsum('tsre,srkde->tsrkd', cot_four, out_halves, precision=highest)
        grad_parts = jnp.einsum('tsrkd,srkc->tscd', backward_terms, out_hot_halves, precision=highest)
        grad_parts = grad_parts.reshape(-1, N_TENSOR, D_OLD).astype(jnp.bfloat16)
        grad_parts = lax.optimization_barrier(grad_parts)
        old_grad = jnp.sum(grad_parts.astype(jnp.float32), axis=1).astype(jnp.bfloat16)
        hidden_grad = jnp.dot(old_grad, mixed_weight.T, preferred_element_type=jnp.float32).astype(jnp.bfloat16)
        grad_selected = jnp.take(hidden_grad.reshape(-1, HG_OLD, HEAD), in_cols, axis=1).astype(jnp.float32)
        grad_attn = jnp.einsum('trke,rkde->trd', grad_selected, in_weights, precision=highest).reshape(-1, F_NEW).astype(jnp.bfloat16)
        in_terms = jnp.einsum('trd,trke->rkde', attn_three, grad_selected, precision=highest)
        cot_three = cot_rows.reshape(-1, BO_NEW, HEAD).astype(jnp.float32)
        out_terms = jnp.einsum('trkd,tre->rkde', old_selected, cot_three, precision=highest)
        return (totals[0] + in_terms, totals[1] + out_terms), (grown, grad_attn)

    attn_split = attn_out.reshape(TOKENS // TOK_DEV, TOK_DEV, F_NEW)
    cot_split = cotangent.reshape(TOKENS // TOK_DEV, TOK_DEV, D_NEW)
    start = (jnp.zeros((HG_NEW, K_IN, HEAD, HEAD), jnp.float32), jnp.zeros((BO_NEW, K_OUT, HEAD, HEAD), jnp.float32))
    sums, outputs = lax.scan(token_block, start, (attn_split, cot_split))
    grad_scale = jnp.float32(TOKENS) ** -0.5
    grown_out = outputs[0].reshape(TOKENS, D_NEW)
    grad_attn = outputs[1].reshape(TOKENS, F_NEW)
    return grown_out, grad_attn, sums[0] * grad_scale, sums[1] * grad_scale
```

```python
import functools

import jax
import jax.numpy as jnp
from jax import lax
from jax.experimental import pallas as pl
from jax.experimental.pallas import tpu as pltpu
from jax.sharding import PartitionSpec as P

HEAD = 128
MESH = pl.DeviceIdType.MESH
F32 = jnp.float32
BF16 = jnp.bfloat16


def dot(a, b, ca=1, cb=0):
    return lax.dot_general(a, b, (((ca,), (cb,)), ((), ())), preferred_element_type=F32)


def kernel(
    dims,
    pick,
    coef,
    in_cols,
    out_cols,
    in_ptr,
    out_ptr,
    attn,
    cot,
    old_w,
    in_b,
    out_b,
    grown,
    gattn,
    terms,
    w_all,
    sums,
    og_mine,
    og_theirs,
    p_mine,
    p_theirs,
    oo,
    hid,
    hg_acc,
    hg_all,
    w_send,
    w_recv,
    og_send,
    og_recv,
    p_send,
    p_recv,
    hg_send,
    hg_recv,
):
    zs, depth_k, k_in, k_out = dims
    shard = w_all.shape[2]
    feats = w_all.shape[1]
    half_rows = feats // 2
    nb = shard // HEAD
    nl = feats // HEAD
    n_out = og_mine.shape[0]
    pairs_in = in_cols.shape[0]
    pairs_out = out_cols.shape[0]
    rows_all = pairs_in // k_in
    rows_out = pairs_out // k_out
    rows_in = gattn.shape[1] // HEAD

    dp = lax.axis_index("dp")
    fs = lax.axis_index("fsdp")
    tn = lax.axis_index("tensor")
    z = fs // 2
    core = fs % 2
    h = dp % 2
    o = 1 - h
    other_core = {"fsdp": 2 * z + 1 - core}
    other_dp = {"dp": dp + 1 - 2 * h}
    other_tn = {"tensor": 1 - tn}
    above = {"fsdp": fs + 2}
    below = {"fsdp": fs - 2}

    def rows_of(half):
        return pl.ds(pl.multiple_of(half * half_rows, half_rows), half_rows)

    def w_copy(f, half, kind, to):
        piece = w_all.at[f, rows_of(half)]
        return pltpu.make_async_remote_copy(
            src_ref=piece,
            dst_ref=piece,
            send_sem=w_send.at[f, half, kind],
            recv_sem=w_recv.at[f, half],
            device_id=to,
            device_id_type=MESH,
        )

    def chunk_copy(src, dst, send, recv, f):
        part = pl.ds(f * nb, nb)
        return pltpu.make_async_remote_copy(
            src_ref=src.at[part],
            dst_ref=dst.at[part],
            send_sem=send.at[f],
            recv_sem=recv.at[f],
            device_id=other_tn,
            device_id_type=MESH,
        )

    def hg_copy(half):
        part = hg_all.at[pl.ds(half * nl, nl)]
        return pltpu.make_async_remote_copy(
            src_ref=part,
            dst_ref=part,
            send_sem=hg_send,
            recv_sem=hg_recv,
            device_id=other_tn,
            device_id_type=MESH,
        )

    barrier = pltpu.get_barrier_semaphore()
    for to in (other_core, other_dp, other_tn):
        pl.semaphore_signal(barrier, inc=1, device_id=to, device_id_type=MESH)

    @pl.when(z > 0)
    def _():
        pl.semaphore_signal(barrier, inc=1, device_id=below, device_id_type=MESH)

    @pl.when(z < zs - 1)
    def _():
        pl.semaphore_signal(barrier, inc=1, device_id=above, device_id_type=MESH)

    inner = (z > 0).astype(jnp.int32) + (z < zs - 1).astype(jnp.int32)
    pl.semaphore_wait(barrier, 3 + inner)

    mix_rows = 64

    def mix(half):
        def body(i, _):
            part = pl.ds(pl.multiple_of(half * half_rows + i * mix_rows, mix_rows), mix_rows)
            total = coef[0] * old_w[pick[0], part, :].astype(F32)
            for j in range(1, depth_k):
                total = total + coef[j] * old_w[pick[j], part, :].astype(F32)
            w_all[fs, part, :] = total.astype(BF16)
            return 0

        lax.fori_loop(0, half_rows // mix_rows, body, 0)

    mix(h)

    @pl.when(z < zs - 1)
    def _():
        w_copy(fs, h, 0, above).start()

    @pl.when(z > 0)
    def _():
        w_copy(fs, h, 1, below).start()

    w_copy(fs, h, 3, other_core).start()
    mix(o)
    w_copy(fs, o, 3, other_core).start()

    sums[pairs_out] = jnp.zeros((HEAD, HEAD), F32)

    def back_row(r, _):
        cols = pl.ds(pl.multiple_of(r * HEAD, HEAD), HEAD)
        for k in range(k_out):
            j = r * k_out + k
            sums[j] = dot(cot[:, cols], out_b[j], 1, 1) + sums[out_ptr[j]]
        return 0

    lax.fori_loop(0, rows_out, back_row, 0, unroll=4)

    def back_block(b, _):
        og_mine[b] = sums[out_ptr[pairs_out + b]].astype(BF16)
        return 0

    lax.fori_loop(0, n_out, back_block, 0, unroll=4)

    def over_shards(s, body):
        def one(i, _):
            zz = z - s + 2 * s * (i // 2)
            cc = (core + i) % 2
            live = (zz >= 0) & (zz < zs) & ((s > 0) | (i < 2))

            @pl.when(live)
            def _():
                body(zz * 2 + cc, i % 2)

            return 0

        lax.fori_loop(0, 4, one, 0)

    def og_start(s, _):
        over_shards(s, lambda f, mine: chunk_copy(og_mine, og_theirs, og_send, og_recv, f).start())
        return 0

    lax.fori_loop(0, zs, og_start, 0)

    sums[pairs_in] = jnp.zeros((HEAD, HEAD), F32)

    def hid_row(r, _):
        cols = pl.ds(pl.multiple_of(r * HEAD, HEAD), HEAD)
        for k in range(k_in):
            j = r * k_in + k
            sums[j] = dot(attn[:, cols], in_b[j]) + sums[in_ptr[j]]
        return 0

    lax.fori_loop(0, rows_all, hid_row, 0, unroll=4)
    for b in range(nl):
        hid[:, b * HEAD : (b + 1) * HEAD] = sums[in_ptr[pairs_in + tn * nl + b]].astype(BF16)

    hg_acc[...] = jnp.zeros_like(hg_acc)

    def forward(f, s):
        part = dot(hid[...], w_all[f]).astype(BF16)
        for b in range(nb):
            p_mine[f * nb + b] = part[:, b * HEAD : (b + 1) * HEAD]
        chunk_copy(p_mine, p_theirs, p_send, p_recv, f).start()

    def backward(f, flip):
        chunk_copy(og_mine, og_theirs, og_send, og_recv, f).wait_recv()
        blocks = [
            (og_mine[f * nb + b].astype(F32) + og_theirs[f * nb + b].astype(F32)).astype(BF16)
            for b in range(nb)
        ]
        hg_acc[...] += dot(jnp.concatenate(blocks, axis=1), w_all[f], 1, 1)

    def step(s, _):
        for way in range(2):
            zz = z - s + 2 * s * way
            nxt = z + 1 - 2 * way
            f = 2 * zz + core

            @pl.when((zz >= 0) & (zz < zs))
            def _():
                w_copy(f, h, way, other_dp).wait_recv()

                @pl.when((nxt >= 0) & (nxt < zs))
                def _():
                    w_copy(f, h, way, above if way == 0 else below).start()

                w_copy(f, h, 2, other_dp).start()
                w_copy(f, h, 3, other_core).start()

        def first(f, flip):
            @pl.when(flip == 1)
            def _():
                w_copy(f, 0, 3, other_core).wait_recv()
                w_copy(f, 1, 3, other_core).wait_recv()

            forward(f, s)

        over_shards(s - 1, first)

        for way in range(2):
            zz = z - s + 2 * s * way
            f = 2 * zz + core

            @pl.when((zz >= 0) & (zz < zs))
            def _():
                w_copy(f, o, 2, other_dp).wait_recv()
                w_copy(f, o, 3, other_core).start()

        @pl.when(s >= 2)
        def _():
            over_shards(s - 2, backward)

        return 0

    lax.fori_loop(1, zs + 2, step, 0)

    for b in range(nl):
        hg_all[tn * nl + b] = hg_acc[:, b * HEAD : (b + 1) * HEAD].astype(BF16)
    hg_copy(tn).start()

    def add_shard(f, _):
        chunk_copy(p_mine, p_theirs, p_send, p_recv, f).wait_recv()
        for b in range(nb):
            oo[f * nb + b] = (
                p_mine[f * nb + b].astype(F32) + p_theirs[f * nb + b].astype(F32)
            ).astype(BF16)
        return 0

    lax.fori_loop(0, 2 * zs, add_shard, 0)

    def out_row(r, _):
        cols = pl.ds(pl.multiple_of(r * HEAD, HEAD), HEAD)
        total = None
        for k in range(k_out):
            j = r * k_out + k
            block = oo[out_cols[j]]
            term = dot(block, out_b[j])
            total = term if total is None else total + term
            terms[j] = dot(block, cot[:, cols], 0, 0).astype(BF16)
        grown[:, cols] = total.astype(BF16)
        return 0

    lax.fori_loop(0, rows_out, out_row, 0, unroll=4)

    hg_copy(1 - tn).wait_recv()

    def in_row(r, _):
        cols = pl.ds(pl.multiple_of(r * HEAD, HEAD), HEAD)
        mine = tn * rows_in + r
        mine_cols = pl.ds(pl.multiple_of(mine * HEAD, HEAD), HEAD)
        total = None
        for k in range(k_in):
            j = mine * k_in + k
            block = hg_all[in_cols[j]]
            term = dot(block, in_b[j], 1, 1)
            total = term if total is None else total + term
            terms[pairs_out + r * k_in + k] = dot(attn[:, mine_cols], block, 0, 0).astype(BF16)
        gattn[:, cols] = total.astype(BF16)
        return 0

    lax.fori_loop(0, rows_in, in_row, 0, unroll=2)

    def send_done(f, _):
        chunk_copy(og_mine, og_theirs, og_send, og_recv, f).wait_send()
        chunk_copy(p_mine, p_theirs, p_send, p_recv, f).wait_send()
        return 0

    lax.fori_loop(0, 2 * zs, send_done, 0)
    hg_copy(tn).wait_send()

    @pl.when(z < zs - 1)
    def _():
        w_copy(fs, h, 0, above).wait_send()

    @pl.when(z > 0)
    def _():
        w_copy(fs, h, 1, below).wait_send()

    w_copy(fs, h, 3, other_core).wait_send()
    w_copy(fs, o, 3, other_core).wait_send()

    def relay_done(s, _):
        for way in range(2):
            zz = z - s + 2 * s * way
            nxt = z + 1 - 2 * way
            f = 2 * zz + core

            @pl.when((zz >= 0) & (zz < zs))
            def _():
                @pl.when((nxt >= 0) & (nxt < zs))
                def _():
                    w_copy(f, h, way, above if way == 0 else below).wait_send()

                w_copy(f, h, 2, other_dp).wait_send()
                w_copy(f, h, 3, other_core).wait_send()
                w_copy(f, o, 3, other_core).wait_send()

        return 0

    lax.fori_loop(1, zs, relay_done, 0)


def chains(cols, targets):
    flat = cols.reshape(-1)
    count = flat.shape[0]
    spot = jnp.arange(count, dtype=jnp.int32)
    want = jnp.concatenate([flat, jnp.arange(targets, dtype=jnp.int32)])
    limit = jnp.concatenate([spot, jnp.full((targets,), count, jnp.int32)])
    same = (want[:, None] == flat[None, :]) & (spot[None, :] < limit[:, None])
    found = jnp.max(jnp.where(same, spot[None, :], -1), axis=1)
    return jnp.where(found < 0, count, found)


def local(
    attn_out,
    cotangent,
    old_weights,
    depth_coef,
    depth_pick,
    in_blocks,
    in_cols,
    out_blocks,
    out_cols,
):
    tok = attn_out.shape[0]
    fsdp = lax.axis_size("fsdp")
    tensor = lax.axis_size("tensor")
    dps = lax.axis_size("dp")
    zs = fsdp // 2
    _, feats, shard = old_weights.shape
    n_out = fsdp * shard // HEAD
    n_in = tensor * feats // HEAD
    rows_all, k_in = in_cols.shape
    rows_out, k_out = out_cols.shape
    rows_in = rows_all // tensor
    pairs_in, pairs_out = rows_all * k_in, rows_out * k_out
    n_terms = pairs_out + rows_in * k_in
    depth_k = depth_pick.shape[0]
    smem = pl.BlockSpec(memory_space=pltpu.SMEM)
    vmem = pl.BlockSpec(memory_space=pltpu.VMEM)
    dma = pltpu.SemaphoreType.DMA
    blocks = (n_out, tok, HEAD)
    grown, gattn, terms = pl.pallas_call(
        functools.partial(kernel, (zs, depth_k, k_in, k_out)),
        out_shape=(
            jax.ShapeDtypeStruct((tok, rows_out * HEAD), BF16),
            jax.ShapeDtypeStruct((tok, rows_in * HEAD), BF16),
            jax.ShapeDtypeStruct((n_terms, HEAD, HEAD), BF16),
        ),
        in_specs=[smem] * 6 + [vmem] * 5,
        out_specs=(vmem, vmem, vmem),
        scratch_shapes=[
            pltpu.VMEM((fsdp, feats, shard), BF16),
            pltpu.VMEM((max(pairs_in, pairs_out) + 1, tok, HEAD), F32),
            pltpu.VMEM(blocks, BF16),
            pltpu.VMEM(blocks, BF16),
            pltpu.VMEM(blocks, BF16),
            pltpu.VMEM(blocks, BF16),
            pltpu.VMEM(blocks, BF16),
            pltpu.VMEM((tok, feats), BF16),
            pltpu.VMEM((tok, feats), F32),
            pltpu.VMEM((n_in, tok, HEAD), BF16),
            dma((fsdp, 2, 4)),
            dma((fsdp, 2)),
            dma((fsdp,)),
            dma((fsdp,)),
            dma((fsdp,)),
            dma((fsdp,)),
            dma,
            dma,
        ],
        compiler_params=pltpu.CompilerParams(
            collective_id=0, has_side_effects=True, vmem_limit_bytes=52 * 2**20
        ),
    )(
        depth_pick,
        depth_coef,
        in_cols.reshape(-1),
        out_cols.reshape(-1),
        chains(in_cols, n_in),
        chains(out_cols, n_out),
        attn_out,
        cotangent,
        old_weights,
        in_blocks.reshape(pairs_in, HEAD, HEAD),
        out_blocks.reshape(pairs_out, HEAD, HEAD),
    )
    total = lax.psum(terms, ("dp", "fsdp")).astype(F32)
    total = total * float(tok * dps * fsdp) ** (-0.5)
    out_sum = total[:pairs_out].reshape(rows_out, k_out, HEAD, HEAD)
    in_sum = total[pairs_out:].reshape(rows_in, k_in, HEAD, HEAD)
    return grown, gattn, in_sum, out_sum


def solution(mesh):
    placed = (
        P(("dp", "fsdp"), None),
        P(("dp", "fsdp"), "tensor"),
        P(None, "tensor", "fsdp"),
        P(),
        P(),
        P(),
        P(),
        P("tensor", None, None, None),
        P("tensor", None),
    )
    return jax.shard_map(
        local,
        mesh=mesh,
        in_specs=placed,
        out_specs=(
            P(("dp", "fsdp"), "tensor"),
            P(("dp", "fsdp"), "tensor"),
            P("tensor", None, None, None),
            P("tensor", None, None, None),
        ),
        check_vma=False,
    )
```

```python
import functools

import jax
import jax.numpy as jnp
from jax import lax
from jax.experimental import pallas as pl
from jax.experimental.pallas import tpu as pltpu
from jax.sharding import PartitionSpec as P

HEAD = 128
MESH = pl.DeviceIdType.MESH
F32 = jnp.float32
BF16 = jnp.bfloat16


def dot(a, b, ca=1, cb=0):
    return lax.dot_general(a, b, (((ca,), (cb,)), ((), ())), preferred_element_type=F32)


def kernel(
    dims,
    pick,
    coef,
    in_cols,
    out_cols,
    in_ptr,
    out_ptr,
    attn,
    cot,
    old_w,
    in_b,
    out_b,
    grown,
    gattn,
    out_sum,
    in_sum,
    w_all,
    sums,
    og_mine,
    og_theirs,
    p_mine,
    p_theirs,
    oo,
    hid,
    hg_acc,
    hg_all,
    w_send,
    w_recv,
    og_send,
    og_recv,
    p_send,
    p_recv,
    hg_send,
    hg_recv,
    *streams,
):
    zs, dps, depth_k, k_in, k_out, scale = dims
    streams = (streams[:14], streams[14:])
    shard = w_all.shape[2]
    feats = w_all.shape[1]
    half_rows = feats // 2
    nb = shard // HEAD
    nl = feats // HEAD
    n_out = og_mine.shape[0]
    pairs_in = in_cols.shape[0]
    pairs_out = out_cols.shape[0]
    rows_all = pairs_in // k_in
    rows_out = pairs_out // k_out
    rows_in = gattn.shape[1] // HEAD

    dp = lax.axis_index("dp")
    fs = lax.axis_index("fsdp")
    tn = lax.axis_index("tensor")
    z = fs // 2
    core = fs % 2
    h = dp % 2
    o = 1 - h
    other_core = {"fsdp": 2 * z + 1 - core}
    other_dp = {"dp": dp + 1 - 2 * h}
    other_tn = {"tensor": 1 - tn}
    above = {"fsdp": fs + 2}
    below = {"fsdp": fs - 2}

    def rows_of(half):
        return pl.ds(pl.multiple_of(half * half_rows, half_rows), half_rows)

    def w_copy(f, half, kind, to):
        piece = w_all.at[f, rows_of(half)]
        return pltpu.make_async_remote_copy(
            src_ref=piece,
            dst_ref=piece,
            send_sem=w_send.at[f, half, kind],
            recv_sem=w_recv.at[f, half],
            device_id=to,
            device_id_type=MESH,
        )

    def chunk_copy(src, dst, send, recv, f):
        part = pl.ds(f * nb, nb)
        return pltpu.make_async_remote_copy(
            src_ref=src.at[part],
            dst_ref=dst.at[part],
            send_sem=send.at[f],
            recv_sem=recv.at[f],
            device_id=other_tn,
            device_id_type=MESH,
        )

    def hg_copy(half):
        part = hg_all.at[pl.ds(half * nl, nl)]
        return pltpu.make_async_remote_copy(
            src_ref=part,
            dst_ref=part,
            send_sem=hg_send,
            recv_sem=hg_recv,
            device_id=other_tn,
            device_id_type=MESH,
        )

    barrier = pltpu.get_barrier_semaphore()
    for to in (other_core, other_tn):
        pl.semaphore_signal(barrier, inc=1, device_id=to, device_id_type=MESH)
    for i in range(1, dps):
        to = {"dp": (dp + i) % dps}
        pl.semaphore_signal(barrier, inc=1, device_id=to, device_id_type=MESH)
    for i in range(1, zs):
        to = {"fsdp": 2 * ((z + i) % zs) + core}
        pl.semaphore_signal(barrier, inc=1, device_id=to, device_id_type=MESH)
    pl.semaphore_wait(barrier, dps + zs)

    mix_rows = 64

    def mix(half):
        def body(i, _):
            part = pl.ds(pl.multiple_of(half * half_rows + i * mix_rows, mix_rows), mix_rows)
            total = coef[0] * old_w[pick[0], part, :].astype(F32)
            for j in range(1, depth_k):
                total = total + coef[j] * old_w[pick[j], part, :].astype(F32)
            w_all[fs, part, :] = total.astype(BF16)
            return 0

        lax.fori_loop(0, half_rows // mix_rows, body, 0)

    mix(h)

    @pl.when(z < zs - 1)
    def _():
        w_copy(fs, h, 0, above).start()

    @pl.when(z > 0)
    def _():
        w_copy(fs, h, 1, below).start()

    w_copy(fs, h, 3, other_core).start()
    mix(o)
    w_copy(fs, o, 3, other_core).start()

    sums[pairs_out] = jnp.zeros((HEAD, HEAD), F32)

    def back_row(r, _):
        cols = pl.ds(pl.multiple_of(r * HEAD, HEAD), HEAD)
        for k in range(k_out):
            j = r * k_out + k
            sums[j] = dot(cot[:, cols], out_b[j], 1, 1) + sums[out_ptr[j]]
        return 0

    lax.fori_loop(0, rows_out, back_row, 0, unroll=4)

    def back_block(b, _):
        og_mine[b] = sums[out_ptr[pairs_out + b]].astype(BF16)
        return 0

    lax.fori_loop(0, n_out, back_block, 0, unroll=4)

    def over_shards(s, body):
        def one(i, _):
            zz = z - s + 2 * s * (i // 2)
            cc = (core + i) % 2
            live = (zz >= 0) & (zz < zs) & ((s > 0) | (i < 2))

            @pl.when(live)
            def _():
                body(zz * 2 + cc, i % 2)

            return 0

        lax.fori_loop(0, 4, one, 0)

    def og_start(s, _):
        over_shards(s, lambda f, mine: chunk_copy(og_mine, og_theirs, og_send, og_recv, f).start())
        return 0

    lax.fori_loop(0, zs, og_start, 0)

    sums[pairs_in] = jnp.zeros((HEAD, HEAD), F32)

    def hid_row(r, _):
        cols = pl.ds(pl.multiple_of(r * HEAD, HEAD), HEAD)
        for k in range(k_in):
            j = r * k_in + k
            sums[j] = dot(attn[:, cols], in_b[j]) + sums[in_ptr[j]]
        return 0

    lax.fori_loop(0, rows_all, hid_row, 0, unroll=4)
    for b in range(nl):
        hid[:, b * HEAD : (b + 1) * HEAD] = sums[in_ptr[pairs_in + tn * nl + b]].astype(BF16)

    hg_acc[...] = jnp.zeros_like(hg_acc)

    def forward(f, s):
        part = dot(hid[...], w_all[f]).astype(BF16)
        for b in range(nb):
            p_mine[f * nb + b] = part[:, b * HEAD : (b + 1) * HEAD]
        chunk_copy(p_mine, p_theirs, p_send, p_recv, f).start()

    def backward(f, flip):
        chunk_copy(og_mine, og_theirs, og_send, og_recv, f).wait_recv()
        blocks = [
            (og_mine[f * nb + b].astype(F32) + og_theirs[f * nb + b].astype(F32)).astype(BF16)
            for b in range(nb)
        ]
        hg_acc[...] += dot(jnp.concatenate(blocks, axis=1), w_all[f], 1, 1)

    def step(s, _):
        for way in range(2):
            zz = z - s + 2 * s * way
            nxt = z + 1 - 2 * way
            f = 2 * zz + core

            @pl.when((zz >= 0) & (zz < zs))
            def _():
                w_copy(f, h, way, other_dp).wait_recv()

                @pl.when((nxt >= 0) & (nxt < zs))
                def _():
                    w_copy(f, h, way, above if way == 0 else below).start()

                w_copy(f, h, 2, other_dp).start()
                w_copy(f, h, 3, other_core).start()

        def first(f, flip):
            @pl.when(flip == 1)
            def _():
                w_copy(f, 0, 3, other_core).wait_recv()
                w_copy(f, 1, 3, other_core).wait_recv()

            forward(f, s)

        over_shards(s - 1, first)

        for way in range(2):
            zz = z - s + 2 * s * way
            f = 2 * zz + core

            @pl.when((zz >= 0) & (zz < zs))
            def _():
                w_copy(f, o, 2, other_dp).wait_recv()
                w_copy(f, o, 3, other_core).start()

        @pl.when(s >= 2)
        def _():
            over_shards(s - 2, backward)

        return 0

    lax.fori_loop(1, zs + 2, step, 0)

    for b in range(nl):
        hg_all[tn * nl + b] = hg_acc[:, b * HEAD : (b + 1) * HEAD].astype(BF16)
    hg_copy(tn).start()

    def piece_copy(src, dst, send, recv, to):
        return pltpu.make_async_remote_copy(
            src_ref=src, dst_ref=dst, send_sem=send, recv_sem=recv, device_id=to, device_id_type=MESH
        )

    class Stream:
        def __init__(self, refs):
            (self.g, self.from_core, self.from_dp, self.from_z, self.full) = refs[:5]
            (self.c_s, self.c_r, self.y_s, self.y_r, self.z_s, self.z_r) = refs[5:11]
            (self.a_r, self.az_s, self.ay_s) = refs[11:14]
            self.u = self.from_z.shape[1]

        def rows(self, c, e, q):
            return pl.ds(pl.multiple_of(((c * dps + e) * zs + q) * self.u, self.u), self.u)

        def core_copy(self, e, q):
            return piece_copy(
                self.g.at[self.rows(1 - core, e, q)],
                self.from_core.at[e * zs + q],
                self.c_s.at[e, q],
                self.c_r.at[e, q],
                other_core,
            )

        def dp_copy(self, src, e, q):
            return piece_copy(
                self.g.at[self.rows(core, e, q)],
                self.from_dp.at[src * zs + q],
                self.y_s.at[e, q],
                self.y_r.at[src, q],
                {"dp": e},
            )

        def z_copy(self, src, q):
            return piece_copy(
                self.g.at[self.rows(core, dp, q)],
                self.from_z.at[src],
                self.z_s.at[q],
                self.z_r.at[src],
                {"fsdp": 2 * q + core},
            )

        def full_copy(self, c, e, q, send, to):
            piece = self.full.at[self.rows(c, e, q)]
            return piece_copy(piece, piece, send, self.a_r.at[c, e, q], to)

        def gather_z(self, q):
            return self.full_copy(core, dp, z, self.az_s.at[q], {"fsdp": 2 * q + core})

        def gather_dp(self, e, q):
            return self.full_copy(core, dp, q, self.ay_s.at[e, q], {"dp": e})

        def gather_core(self, e, q):
            return self.full_copy(core, e, q, self.c_s.at[e, q], other_core)

        def came(self, c, e, q):
            self.full_copy(c, e, q, self.c_s.at[e, q], other_core).wait_recv()

        def each_q(self, body):
            def one(i, _):
                body((z + 1 + i) % zs)
                return 0

            lax.fori_loop(0, zs, one, 0)

        def each_e(self, body, own=False):
            def one(i, _):
                body((dp + 1 + i) % dps)
                return 0

            lax.fori_loop(0, dps if own else dps - 1, one, 0)

        def start_core(self):
            self.each_e(lambda e: self.each_q(lambda q: self.core_copy(e, q).start()), True)

        def core_sums(self):
            def one(e, q):
                self.core_copy(e, q).wait()
                rows = self.rows(core, e, q)
                total = self.g[rows, :].astype(F32) + self.from_core[e * zs + q].astype(F32)
                self.g[rows, :] = total.astype(BF16)

                @pl.when(e != dp)
                def _():
                    self.dp_copy(dp, e, q).start()

            self.each_e(lambda e: self.each_q(lambda q: one(e, q)), True)

        def dp_sums(self):
            def one(q):
                rows = self.rows(core, dp, q)
                total = self.g[rows, :].astype(F32)
                for i in range(1, dps):
                    src = (dp + i) % dps
                    self.dp_copy(src, dp, q).wait_recv()
                    total = total + self.from_dp[src * zs + q].astype(F32)
                self.g[rows, :] = total.astype(BF16)

                @pl.when(q != z)
                def _():
                    self.z_copy(z, q).start()

            self.each_q(one)

        def z_sums(self):
            total = self.g[self.rows(core, dp, z), :].astype(F32)
            for i in range(1, zs):
                src = (z + i) % zs
                self.z_copy(src, z).wait_recv()
                total = total + self.from_z[src].astype(F32)
            self.full[self.rows(core, dp, z), :] = total.astype(BF16)

            def to_z(i, _):
                self.gather_z((z + i) % zs).start()
                return 0

            lax.fori_loop(1, zs, to_z, 0)
            self.each_e(lambda e: self.gather_dp(e, z).start())
            self.gather_core(dp, z).start()

        def near(self, body):
            def one(s, _):
                for zz in (z - s, z + s):
                    @pl.when((zz >= 0) & (zz < zs))
                    def _():
                        body(zz)

                return 0

            lax.fori_loop(1, zs, one, 0)

        def forward_z(self):
            def one(q):
                self.came(core, dp, q)
                self.each_e(lambda e: self.gather_dp(e, q).start())
                self.gather_core(dp, q).start()

            self.near(one)

        def forward_dp(self):
            def one(q):
                def each(e):
                    self.came(core, e, q)
                    self.gather_core(e, q).start()

                self.each_e(each)

            one(z)
            self.near(one)

        def finish(self, result):
            self.each_e(lambda e: self.each_q(lambda q: self.came(1 - core, e, q)), True)

            def block(i, _):
                rows = pl.ds(pl.multiple_of(i * HEAD, HEAD), HEAD)
                result[i] = self.full[rows, :].astype(F32) * scale
                return 0

            lax.fori_loop(0, result.shape[0], block, 0)

        def drain(self):
            self.each_e(lambda e: self.each_q(lambda q: self.dp_copy(dp, e, q).wait_send()))
            self.each_e(lambda e: self.each_q(lambda q: self.gather_dp(e, q).wait_send()))
            self.each_e(lambda e: self.each_q(lambda q: self.gather_core(e, q).wait_send()), True)

            def to_z(i, _):
                self.z_copy(z, (z + i) % zs).wait_send()
                self.gather_z((z + i) % zs).wait_send()
                return 0

            lax.fori_loop(1, zs, to_z, 0)

        def clear_tail(self, used):
            spare = self.g.shape[0] - used
            if spare > 0:
                self.g[used:, :] = jnp.zeros((spare, HEAD), BF16)

    outs, ins = Stream(streams[0]), Stream(streams[1])
    outs.clear_tail(pairs_out * HEAD)
    ins.clear_tail(rows_in * k_in * HEAD)

    def add_shard(f, _):
        chunk_copy(p_mine, p_theirs, p_send, p_recv, f).wait_recv()
        for b in range(nb):
            oo[f * nb + b] = (
                p_mine[f * nb + b].astype(F32) + p_theirs[f * nb + b].astype(F32)
            ).astype(BF16)
        return 0

    lax.fori_loop(0, 2 * zs, add_shard, 0)

    def out_row(r, _):
        cols = pl.ds(pl.multiple_of(r * HEAD, HEAD), HEAD)
        for k in range(k_out):
            j = r * k_out + k
            to = pl.ds(pl.multiple_of(j * HEAD, HEAD), HEAD)
            outs.g[to, :] = dot(oo[out_cols[j]], cot[:, cols], 0, 0).astype(BF16)
        return 0

    lax.fori_loop(0, rows_out, out_row, 0, unroll=4)
    outs.start_core()
    hg_copy(1 - tn).wait_recv()

    def in_row(r, _):
        mine = tn * rows_in + r
        mine_cols = pl.ds(pl.multiple_of(mine * HEAD, HEAD), HEAD)
        for k in range(k_in):
            block = hg_all[in_cols[mine * k_in + k]]
            to = pl.ds(pl.multiple_of((r * k_in + k) * HEAD, HEAD), HEAD)
            ins.g[to, :] = dot(attn[:, mine_cols], block, 0, 0).astype(BF16)
        return 0

    lax.fori_loop(0, rows_in, in_row, 0, unroll=2)
    ins.start_core()
    outs.core_sums()
    ins.core_sums()

    def grown_row(r, _):
        cols = pl.ds(pl.multiple_of(r * HEAD, HEAD), HEAD)
        total = None
        for k in range(k_out):
            j = r * k_out + k
            term = dot(oo[out_cols[j]], out_b[j])
            total = term if total is None else total + term
        grown[:, cols] = total.astype(BF16)
        return 0

    lax.fori_loop(0, rows_out, grown_row, 0, unroll=4)
    outs.dp_sums()

    def gattn_row(r, _):
        cols = pl.ds(pl.multiple_of(r * HEAD, HEAD), HEAD)
        total = None
        for k in range(k_in):
            j = (tn * rows_in + r) * k_in + k
            term = dot(hg_all[in_cols[j]], in_b[j], 1, 1)
            total = term if total is None else total + term
        gattn[:, cols] = total.astype(BF16)
        return 0

    lax.fori_loop(0, rows_in, gattn_row, 0, unroll=2)
    ins.dp_sums()
    outs.z_sums()
    ins.z_sums()
    outs.forward_z()
    ins.forward_z()
    outs.forward_dp()
    ins.forward_dp()
    outs.finish(out_sum)
    ins.finish(in_sum)
    outs.drain()
    ins.drain()

    def send_done(f, _):
        chunk_copy(og_mine, og_theirs, og_send, og_recv, f).wait_send()
        chunk_copy(p_mine, p_theirs, p_send, p_recv, f).wait_send()
        return 0

    lax.fori_loop(0, 2 * zs, send_done, 0)
    hg_copy(tn).wait_send()

    @pl.when(z < zs - 1)
    def _():
        w_copy(fs, h, 0, above).wait_send()

    @pl.when(z > 0)
    def _():
        w_copy(fs, h, 1, below).wait_send()

    w_copy(fs, h, 3, other_core).wait_send()
    w_copy(fs, o, 3, other_core).wait_send()

    def relay_done(s, _):
        for way in range(2):
            zz = z - s + 2 * s * way
            nxt = z + 1 - 2 * way
            f = 2 * zz + core

            @pl.when((zz >= 0) & (zz < zs))
            def _():
                @pl.when((nxt >= 0) & (nxt < zs))
                def _():
                    w_copy(f, h, way, above if way == 0 else below).wait_send()

                w_copy(f, h, 2, other_dp).wait_send()
                w_copy(f, h, 3, other_core).wait_send()
                w_copy(f, o, 3, other_core).wait_send()

        return 0

    lax.fori_loop(1, zs, relay_done, 0)


def chains(cols, targets):
    flat = cols.reshape(-1)
    count = flat.shape[0]
    spot = jnp.arange(count, dtype=jnp.int32)
    want = jnp.concatenate([flat, jnp.arange(targets, dtype=jnp.int32)])
    limit = jnp.concatenate([spot, jnp.full((targets,), count, jnp.int32)])
    same = (want[:, None] == flat[None, :]) & (spot[None, :] < limit[:, None])
    found = jnp.max(jnp.where(same, spot[None, :], -1), axis=1)
    return jnp.where(found < 0, count, found)


def local(
    attn_out,
    cotangent,
    old_weights,
    depth_coef,
    depth_pick,
    in_blocks,
    in_cols,
    out_blocks,
    out_cols,
):
    tok = attn_out.shape[0]
    fsdp = lax.axis_size("fsdp")
    tensor = lax.axis_size("tensor")
    dps = lax.axis_size("dp")
    zs = fsdp // 2
    _, feats, shard = old_weights.shape
    n_out = fsdp * shard // HEAD
    n_in = tensor * feats // HEAD
    rows_all, k_in = in_cols.shape
    rows_out, k_out = out_cols.shape
    rows_in = rows_all // tensor
    pairs_in, pairs_out = rows_all * k_in, rows_out * k_out
    depth_k = depth_pick.shape[0]
    smem = pl.BlockSpec(memory_space=pltpu.SMEM)
    vmem = pl.BlockSpec(memory_space=pltpu.VMEM)
    dma = pltpu.SemaphoreType.DMA
    blocks = (n_out, tok, HEAD)
    scale = float(tok * dps * fsdp) ** (-0.5)

    def stream_scratch(rows):
        u = -(-rows // (2 * dps * zs * 16)) * 16
        return [
            pltpu.VMEM((2 * dps * zs * u, HEAD), BF16),
            pltpu.VMEM((dps * zs, u, HEAD), BF16),
            pltpu.VMEM((dps * zs, u, HEAD), BF16),
            pltpu.VMEM((zs, u, HEAD), BF16),
            pltpu.VMEM((2 * dps * zs * u, HEAD), BF16),
            dma((dps, zs)),
            dma((dps, zs)),
            dma((dps, zs)),
            dma((dps, zs)),
            dma((zs,)),
            dma((zs,)),
            dma((2, dps, zs)),
            dma((zs,)),
            dma((dps, zs)),
        ]

    grown, gattn, out_sum, in_sum = pl.pallas_call(
        functools.partial(kernel, (zs, dps, depth_k, k_in, k_out, scale)),
        out_shape=(
            jax.ShapeDtypeStruct((tok, rows_out * HEAD), BF16),
            jax.ShapeDtypeStruct((tok, rows_in * HEAD), BF16),
            jax.ShapeDtypeStruct((pairs_out, HEAD, HEAD), F32),
            jax.ShapeDtypeStruct((rows_in * k_in, HEAD, HEAD), F32),
        ),
        in_specs=[smem] * 6 + [vmem] * 5,
        out_specs=(vmem, vmem, vmem, vmem),
        scratch_shapes=[
            pltpu.VMEM((fsdp, feats, shard), BF16),
            pltpu.VMEM((max(pairs_in, pairs_out) + 1, tok, HEAD), F32),
            pltpu.VMEM(blocks, BF16),
            pltpu.VMEM(blocks, BF16),
            pltpu.VMEM(blocks, BF16),
            pltpu.VMEM(blocks, BF16),
            pltpu.VMEM(blocks, BF16),
            pltpu.VMEM((tok, feats), BF16),
            pltpu.VMEM((tok, feats), F32),
            pltpu.VMEM((n_in, tok, HEAD), BF16),
            dma((fsdp, 2, 4)),
            dma((fsdp, 2)),
            dma((fsdp,)),
            dma((fsdp,)),
            dma((fsdp,)),
            dma((fsdp,)),
            dma,
            dma,
            *stream_scratch(pairs_out * HEAD),
            *stream_scratch(rows_in * k_in * HEAD),
        ],
        compiler_params=pltpu.CompilerParams(
            collective_id=0, has_side_effects=True, vmem_limit_bytes=52 * 2**20
        ),
    )(
        depth_pick,
        depth_coef,
        in_cols.reshape(-1),
        out_cols.reshape(-1),
        chains(in_cols, n_in),
        chains(out_cols, n_out),
        attn_out,
        cotangent,
        old_weights,
        in_blocks.reshape(pairs_in, HEAD, HEAD),
        out_blocks.reshape(pairs_out, HEAD, HEAD),
    )
    in_sum = in_sum.reshape(rows_in, k_in, HEAD, HEAD)
    out_sum = out_sum.reshape(rows_out, k_out, HEAD, HEAD)
    return grown, gattn, in_sum, out_sum


def solution(mesh):
    placed = (
        P(("dp", "fsdp"), None),
        P(("dp", "fsdp"), "tensor"),
        P(None, "tensor", "fsdp"),
        P(),
        P(),
        P(),
        P(),
        P("tensor", None, None, None),
        P("tensor", None),
    )
    return jax.shard_map(
        local,
        mesh=mesh,
        in_specs=placed,
        out_specs=(
            P(("dp", "fsdp"), "tensor"),
            P(("dp", "fsdp"), "tensor"),
            P("tensor", None, None, None),
            P("tensor", None, None, None),
        ),
        check_vma=False,
    )
```

```python
import functools

import jax
import jax.numpy as jnp
from jax import lax
from jax.experimental import pallas as pl
from jax.experimental.pallas import tpu as pltpu
from jax.sharding import PartitionSpec as P

HEAD = 128
MESH = pl.DeviceIdType.MESH
F32 = jnp.float32
BF16 = jnp.bfloat16


def dot(a, b, ca=1, cb=0):
    return lax.dot_general(a, b, (((ca,), (cb,)), ((), ())), preferred_element_type=F32)


def kernel(
    dims,
    table,
    coef,
    attn_hbm,
    cot_hbm,
    old_w_hbm,
    in_b_hbm,
    out_b_hbm,
    grown,
    gattn,
    out_full,
    in_full,
    attn,
    cot,
    old_w_first,
    old_w_last,
    in_b,
    out_b,
    load_sem,
    w_all,
    sums,
    og_mine,
    og_theirs,
    p_mine,
    p_theirs,
    oo,
    hid,
    hg_acc,
    hg_all,
    w_send,
    w_recv,
    og_send,
    og_recv,
    p_send,
    p_recv,
    hg_send,
    hg_recv,
    *streams,
):
    zs, dps, depth_k, k_in, k_out, rows_all, rows_out, pairs, n_sub = dims
    streams = (streams[:13], streams[13:])
    shard = w_all.shape[2]
    feats = w_all.shape[1]
    half_rows = feats // 2
    nb = shard // HEAD
    nl = feats // HEAD
    n_out = og_mine.shape[0]
    sub_rows = half_rows // n_sub
    pairs_in = rows_all * k_in
    pairs_out = rows_out * k_out
    targets = (table.shape[0] - depth_k) // 2 - 2 * pairs

    def in_col(r, k):
        return table[depth_k + k * rows_all + r]

    def out_col(r, k):
        return table[depth_k + pairs + k * rows_out + r]

    def in_link(i):
        return table[depth_k + 2 * pairs + i]

    def out_link(i):
        return table[depth_k + 3 * pairs + targets + i]

    def load(i, src, dst):
        return pltpu.make_async_copy(src, dst, load_sem.at[i])

    def load_mix(half, i, dst):
        part = pl.ds(pl.multiple_of(half * half_rows, half_rows), half_rows)
        return load(i, old_w_hbm.at[:, part], dst)

    others = [
        load(2, cot_hbm, cot),
        load(3, out_b_hbm, out_b),
        load(4, attn_hbm, attn),
        load(5, in_b_hbm, in_b),
    ]
    rows_in = gattn.shape[1] // HEAD

    dp = lax.axis_index("dp")
    fs = lax.axis_index("fsdp")
    tn = lax.axis_index("tensor")
    z = fs // 2
    core = fs % 2
    h = dp % 2
    o = 1 - h
    other_core = {"fsdp": 2 * z + 1 - core}
    other_dp = {"dp": dp + 1 - 2 * h}
    other_tn = {"tensor": 1 - tn}
    above = {"fsdp": fs + 2}
    below = {"fsdp": fs - 2}

    load_first = load_mix(h, 0, old_w_first)
    load_last = load_mix(o, 1, old_w_last)
    load_first.start()
    load_last.start()
    for one_load in others:
        one_load.start()

    def w_copy(f, half, sub, kind, to):
        start = pl.multiple_of(half * half_rows + sub * sub_rows, sub_rows)
        piece = w_all.at[f, pl.ds(start, sub_rows)]
        return pltpu.make_async_remote_copy(
            src_ref=piece,
            dst_ref=piece,
            send_sem=w_send.at[f, half, sub, kind],
            recv_sem=w_recv.at[f, half, sub],
            device_id=to,
            device_id_type=MESH,
        )

    def chunk_copy(src, dst, send, recv, f):
        part = pl.ds(f * nb, nb)
        return pltpu.make_async_remote_copy(
            src_ref=src.at[part],
            dst_ref=dst.at[part],
            send_sem=send.at[f],
            recv_sem=recv.at[f],
            device_id=other_tn,
            device_id_type=MESH,
        )

    def hg_copy(half):
        part = hg_all.at[pl.ds(half * nl, nl)]
        return pltpu.make_async_remote_copy(
            src_ref=part,
            dst_ref=part,
            send_sem=hg_send,
            recv_sem=hg_recv,
            device_id=other_tn,
            device_id_type=MESH,
        )

    barrier = pltpu.get_barrier_semaphore()
    for to in (other_core, other_tn):
        pl.semaphore_signal(barrier, inc=1, device_id=to, device_id_type=MESH)
    for i in range(1, dps):
        to = {"dp": (dp + i) % dps}
        pl.semaphore_signal(barrier, inc=1, device_id=to, device_id_type=MESH)
    for i in range(1, zs):
        to = {"fsdp": 2 * ((z + i) % zs) + core}
        pl.semaphore_signal(barrier, inc=1, device_id=to, device_id_type=MESH)
    pl.semaphore_wait(barrier, dps + zs)

    mix_rows = 64

    def mix(half, old_w, sub):
        def body(i, _):
            start = sub * sub_rows + i * mix_rows
            part = pl.ds(pl.multiple_of(start, mix_rows), mix_rows)
            to = pl.ds(pl.multiple_of(half * half_rows + start, mix_rows), mix_rows)
            total = coef[0] * old_w[table[0], part, :].astype(F32)
            for j in range(1, depth_k):
                total = total + coef[j] * old_w[table[j], part, :].astype(F32)
            w_all[fs, to, :] = total.astype(BF16)
            return 0

        lax.fori_loop(0, sub_rows // mix_rows, body, 0)

    load_first.wait()

    def first_half(q, _):
        mix(h, old_w_first, q)

        @pl.when(z < zs - 1)
        def _():
            w_copy(fs, h, q, 0, above).start()

        @pl.when(z > 0)
        def _():
            w_copy(fs, h, q, 1, below).start()

        w_copy(fs, h, q, 3, other_core).start()
        return 0

    lax.fori_loop(0, n_sub, first_half, 0)
    load_last.wait()

    def second_half(q, _):
        mix(o, old_w_last, q)
        w_copy(fs, o, q, 3, other_core).start()
        return 0

    lax.fori_loop(0, n_sub, second_half, 0)
    others[0].wait()
    others[1].wait()

    sums[pairs] = jnp.zeros((HEAD, HEAD), F32)

    def back_row(r, _):
        cols = pl.ds(pl.multiple_of(r * HEAD, HEAD), HEAD)
        for k in range(k_out):
            j = r * k_out + k
            sums[j] = dot(cot[:, cols], out_b[j], 1, 1) + sums[out_link(k * rows_out + r)]
        return 0

    lax.fori_loop(0, rows_out, back_row, 0, unroll=4)

    def back_block(b, _):
        og_mine[b] = sums[out_link(pairs + b)].astype(BF16)
        return 0

    lax.fori_loop(0, n_out, back_block, 0, unroll=4)

    def shard_of(s, i, body):
        zz = z - s + 2 * s * (i // 2)
        cc = (core + i) % 2
        live = (zz >= 0) & (zz < zs) & ((s > 0) | (i < 2))

        @pl.when(live)
        def _():
            body(zz * 2 + cc, i % 2)

    def over_shards(s, body):
        def one(i, _):
            shard_of(s, i, body)
            return 0

        lax.fori_loop(0, 4, one, 0)

    def og_start(s, _):
        over_shards(s, lambda f, mine: chunk_copy(og_mine, og_theirs, og_send, og_recv, f).start())
        return 0

    lax.fori_loop(0, zs, og_start, 0)

    others[2].wait()
    others[3].wait()

    def hid_row(r, _):
        cols = pl.ds(pl.multiple_of(r * HEAD, HEAD), HEAD)
        for k in range(k_in):
            j = r * k_in + k
            sums[j] = dot(attn[:, cols], in_b[j]) + sums[in_link(k * rows_all + r)]
        return 0

    lax.fori_loop(0, rows_all, hid_row, 0, unroll=4)
    for b in range(nl):
        hid[:, b * HEAD : (b + 1) * HEAD] = sums[in_link(pairs + tn * nl + b)].astype(BF16)

    hg_acc[...] = jnp.zeros_like(hg_acc)

    def forward(f):
        part = dot(hid[...], w_all[f]).astype(BF16)
        for b in range(nb):
            p_mine[f * nb + b] = part[:, b * HEAD : (b + 1) * HEAD]
        chunk_copy(p_mine, p_theirs, p_send, p_recv, f).start()

    def backward(f, flip):
        chunk_copy(og_mine, og_theirs, og_send, og_recv, f).wait_recv()
        blocks = [
            (og_mine[f * nb + b].astype(F32) + og_theirs[f * nb + b].astype(F32)).astype(BF16)
            for b in range(nb)
        ]
        hg_acc[...] += dot(jnp.concatenate(blocks, axis=1), w_all[f], 1, 1)

    def first(f, flip):
        @pl.when(flip == 1)
        def _():
            def came(q, _):
                w_copy(f, 0, q, 3, other_core).wait_recv()
                w_copy(f, 1, q, 3, other_core).wait_recv()
                return 0

            lax.fori_loop(0, n_sub, came, 0)

        forward(f)

    def relay(s, q):
        for way in range(2):
            zz = z - s + 2 * s * way
            nxt = z + 1 - 2 * way
            f = 2 * zz + core

            @pl.when((zz >= 0) & (zz < zs))
            def _():
                w_copy(f, h, q, way, other_dp).wait_recv()

                @pl.when((nxt >= 0) & (nxt < zs))
                def _():
                    w_copy(f, h, q, way, above if way == 0 else below).start()

                w_copy(f, h, q, 2, other_dp).start()
                w_copy(f, h, q, 3, other_core).start()

    def pass_on(s, q):
        for way in range(2):
            zz = z - s + 2 * s * way
            f = 2 * zz + core

            @pl.when((zz >= 0) & (zz < zs) & (s > 0))
            def _():
                w_copy(f, o, q, 2, other_dp).wait_recv()
                w_copy(f, o, q, 3, other_core).start()

    def step(s, _):
        def part(q, _):
            relay(s, q)
            pass_on(s - (q == 0).astype(jnp.int32), (q + n_sub - 1) % n_sub)
            shard_of(s - 1, q, first)

            @pl.when((s >= 2) & (s < zs))
            def _():
                shard_of(s - 1, q, backward)

            @pl.when(s == 2)
            def _():
                shard_of(0, q, backward)

            return 0

        lax.fori_loop(0, n_sub, part, 0)
        return 0

    lax.fori_loop(1, zs + 1, step, 0)
    over_shards(zs - 1, backward)

    for b in range(nl):
        hg_all[tn * nl + b] = hg_acc[:, b * HEAD : (b + 1) * HEAD].astype(BF16)
    hg_copy(tn).start()

    def piece_copy(src, dst, send, recv, to):
        return pltpu.make_async_remote_copy(
            src_ref=src, dst_ref=dst, send_sem=send, recv_sem=recv, device_id=to, device_id_type=MESH
        )

    class Stream:
        def __init__(self, refs, full):
            (self.g, self.from_core, self.from_dp, self.from_z) = refs[:4]
            (self.c_s, self.c_r, self.y_s, self.y_r, self.z_s, self.z_r) = refs[4:10]
            (self.a_r, self.az_s, self.ay_s) = refs[10:13]
            self.full = full
            self.u = self.from_z.shape[1]

        def rows(self, c, e, q):
            return pl.ds(pl.multiple_of(((c * dps + e) * zs + q) * self.u, self.u), self.u)

        def core_copy(self, e, q):
            return piece_copy(
                self.g.at[self.rows(1 - core, e, q)],
                self.from_core.at[e * zs + q],
                self.c_s.at[e, q],
                self.c_r.at[e, q],
                other_core,
            )

        def dp_copy(self, src, e, q):
            return piece_copy(
                self.g.at[self.rows(core, e, q)],
                self.from_dp.at[src * zs + q],
                self.y_s.at[e, q],
                self.y_r.at[src, q],
                {"dp": e},
            )

        def z_copy(self, src, q):
            return piece_copy(
                self.g.at[self.rows(core, dp, q)],
                self.from_z.at[src],
                self.z_s.at[q],
                self.z_r.at[src],
                {"fsdp": 2 * q + core},
            )

        def full_copy(self, c, e, q, send, to):
            piece = self.full.at[self.rows(c, e, q)]
            return piece_copy(piece, piece, send, self.a_r.at[c, e, q], to)

        def gather_z(self, q):
            return self.full_copy(core, dp, z, self.az_s.at[q], {"fsdp": 2 * q + core})

        def gather_dp(self, e, q):
            return self.full_copy(core, dp, q, self.ay_s.at[e, q], {"dp": e})

        def gather_core(self, e, q):
            return self.full_copy(core, e, q, self.c_s.at[e, q], other_core)

        def came(self, c, e, q):
            self.full_copy(c, e, q, self.c_s.at[e, q], other_core).wait_recv()

        def each_q(self, body):
            def one(i, _):
                body((z + 1 + i) % zs)
                return 0

            lax.fori_loop(0, zs, one, 0)

        def each_e(self, body, own=False):
            def one(i, _):
                body((dp + 1 + i) % dps)
                return 0

            lax.fori_loop(0, dps if own else dps - 1, one, 0)

        def start_core(self):
            self.each_e(lambda e: self.each_q(lambda q: self.core_copy(e, q).start()), True)

        def core_sums(self):
            def one(e, q):
                self.core_copy(e, q).wait()
                rows = self.rows(core, e, q)
                total = self.g[rows, :].astype(F32) + self.from_core[e * zs + q].astype(F32)
                self.g[rows, :] = total.astype(BF16)

                @pl.when(e != dp)
                def _():
                    self.dp_copy(dp, e, q).start()

            self.each_e(lambda e: self.each_q(lambda q: one(e, q)), True)

        def dp_sums(self):
            def one(q):
                rows = self.rows(core, dp, q)
                total = self.g[rows, :].astype(F32)
                for i in range(1, dps):
                    src = (dp + i) % dps
                    self.dp_copy(src, dp, q).wait_recv()
                    total = total + self.from_dp[src * zs + q].astype(F32)
                self.g[rows, :] = total.astype(BF16)

                @pl.when(q != z)
                def _():
                    self.z_copy(z, q).start()

            self.each_q(one)

        def z_sums(self):
            total = self.g[self.rows(core, dp, z), :].astype(F32)
            for i in range(1, zs):
                src = (z + i) % zs
                self.z_copy(src, z).wait_recv()
                total = total + self.from_z[src].astype(F32)
            self.full[self.rows(core, dp, z), :] = total.astype(BF16)

            def to_z(i, _):
                self.gather_z((z + i) % zs).start()
                return 0

            lax.fori_loop(1, zs, to_z, 0)
            self.each_e(lambda e: self.gather_dp(e, z).start())
            self.gather_core(dp, z).start()

        def near(self, body):
            def one(s, _):
                for zz in (z - s, z + s):
                    @pl.when((zz >= 0) & (zz < zs))
                    def _():
                        body(zz)

                return 0

            lax.fori_loop(1, zs, one, 0)

        def forward_z(self):
            def one(q):
                self.came(core, dp, q)
                self.each_e(lambda e: self.gather_dp(e, q).start())
                self.gather_core(dp, q).start()

            self.near(one)

        def forward_dp(self):
            def one(q):
                def each(e):
                    self.came(core, e, q)
                    self.gather_core(e, q).start()

                self.each_e(each)

            one(z)
            self.near(one)

        def finish(self):
            self.each_e(lambda e: self.each_q(lambda q: self.came(1 - core, e, q)), True)

        def drain(self):
            self.each_e(lambda e: self.each_q(lambda q: self.dp_copy(dp, e, q).wait_send()))
            self.each_e(lambda e: self.each_q(lambda q: self.gather_dp(e, q).wait_send()))
            self.each_e(lambda e: self.each_q(lambda q: self.gather_core(e, q).wait_send()), True)

            def to_z(i, _):
                self.z_copy(z, (z + i) % zs).wait_send()
                self.gather_z((z + i) % zs).wait_send()
                return 0

            lax.fori_loop(1, zs, to_z, 0)

        def clear_tail(self, used):
            spare = self.g.shape[0] - used
            if spare > 0:
                self.g[used:, :] = jnp.zeros((spare, HEAD), BF16)

    outs, ins = Stream(streams[0], out_full), Stream(streams[1], in_full)
    outs.clear_tail(pairs_out * HEAD)
    ins.clear_tail(rows_in * k_in * HEAD)

    def add_shard(f, _):
        chunk_copy(p_mine, p_theirs, p_send, p_recv, f).wait_recv()
        for b in range(nb):
            oo[f * nb + b] = (
                p_mine[f * nb + b].astype(F32) + p_theirs[f * nb + b].astype(F32)
            ).astype(BF16)
        return 0

    lax.fori_loop(0, 2 * zs, add_shard, 0)

    def out_row(r, _):
        cols = pl.ds(pl.multiple_of(r * HEAD, HEAD), HEAD)
        for k in range(k_out):
            j = r * k_out + k
            to = pl.ds(pl.multiple_of(j * HEAD, HEAD), HEAD)
            outs.g[to, :] = dot(oo[out_col(r, k)], cot[:, cols], 0, 0).astype(BF16)
        return 0

    lax.fori_loop(0, rows_out, out_row, 0, unroll=4)
    outs.start_core()
    hg_copy(1 - tn).wait_recv()

    def in_row(r, _):
        mine = tn * rows_in + r
        mine_cols = pl.ds(pl.multiple_of(mine * HEAD, HEAD), HEAD)
        for k in range(k_in):
            block = hg_all[in_col(mine, k)]
            to = pl.ds(pl.multiple_of((r * k_in + k) * HEAD, HEAD), HEAD)
            ins.g[to, :] = dot(attn[:, mine_cols], block, 0, 0).astype(BF16)
        return 0

    lax.fori_loop(0, rows_in, in_row, 0, unroll=2)
    ins.start_core()
    outs.core_sums()
    ins.core_sums()

    def grown_row(r, _):
        cols = pl.ds(pl.multiple_of(r * HEAD, HEAD), HEAD)
        total = None
        for k in range(k_out):
            j = r * k_out + k
            term = dot(oo[out_col(r, k)], out_b[j])
            total = term if total is None else total + term
        grown[:, cols] = total.astype(BF16)
        return 0

    lax.fori_loop(0, rows_out, grown_row, 0, unroll=4)
    outs.dp_sums()

    def gattn_row(r, _):
        cols = pl.ds(pl.multiple_of(r * HEAD, HEAD), HEAD)
        total = None
        for k in range(k_in):
            j = (tn * rows_in + r) * k_in + k
            term = dot(hg_all[in_col(tn * rows_in + r, k)], in_b[j], 1, 1)
            total = term if total is None else total + term
        gattn[:, cols] = total.astype(BF16)
        return 0

    lax.fori_loop(0, rows_in, gattn_row, 0, unroll=2)
    ins.dp_sums()
    outs.z_sums()
    ins.z_sums()
    outs.forward_z()
    ins.forward_z()
    outs.forward_dp()
    ins.forward_dp()
    outs.finish()
    ins.finish()
    outs.drain()
    ins.drain()

    def send_done(f, _):
        chunk_copy(og_mine, og_theirs, og_send, og_recv, f).wait_send()
        chunk_copy(p_mine, p_theirs, p_send, p_recv, f).wait_send()
        return 0

    lax.fori_loop(0, 2 * zs, send_done, 0)
    hg_copy(tn).wait_send()

    def own_done(q, _):
        @pl.when(z < zs - 1)
        def _():
            w_copy(fs, h, q, 0, above).wait_send()

        @pl.when(z > 0)
        def _():
            w_copy(fs, h, q, 1, below).wait_send()

        w_copy(fs, h, q, 3, other_core).wait_send()
        w_copy(fs, o, q, 3, other_core).wait_send()
        return 0

    lax.fori_loop(0, n_sub, own_done, 0)

    def relay_done(i, _):
        s = 1 + i // n_sub
        q = i % n_sub
        for way in range(2):
            zz = z - s + 2 * s * way
            nxt = z + 1 - 2 * way
            f = 2 * zz + core

            @pl.when((zz >= 0) & (zz < zs))
            def _():
                @pl.when((nxt >= 0) & (nxt < zs))
                def _():
                    w_copy(f, h, q, way, above if way == 0 else below).wait_send()

                w_copy(f, h, q, 2, other_dp).wait_send()
                w_copy(f, h, q, 3, other_core).wait_send()
                w_copy(f, o, q, 3, other_core).wait_send()

        return 0

    lax.fori_loop(0, (zs - 1) * n_sub, relay_done, 0)


def index_table(pick, in_cols, out_cols, targets):
    pairs = max(in_cols.size, out_cols.size)
    flats, orders = [], []
    for cols in (in_cols, out_cols):
        rows, terms = cols.shape
        short = (0, pairs - cols.size)
        order = jnp.arange(rows, dtype=jnp.int32)[None, :] * terms
        order = order + jnp.arange(terms, dtype=jnp.int32)[:, None]
        flats.append(jnp.pad(cols.T.reshape(-1), short, constant_values=-1))
        orders.append(jnp.pad(order.reshape(-1), short, constant_values=pairs))
    flat, order = jnp.stack(flats), jnp.stack(orders)
    named = jnp.broadcast_to(jnp.arange(targets, dtype=jnp.int32), (2, targets))
    want = jnp.concatenate([flat, named], axis=1)
    limit = jnp.concatenate([order, jnp.full((2, targets), pairs, jnp.int32)], axis=1)
    same = (want[:, :, None] == flat[:, None, :]) & (order[:, None, :] < limit[:, :, None])
    found = jnp.max(jnp.where(same, order[:, None, :], -1), axis=2)
    found = jnp.where(found < 0, pairs, found)
    return jnp.concatenate([pick, flat.reshape(-1), found.reshape(-1)])


def local(
    attn_out,
    cotangent,
    old_weights,
    depth_coef,
    depth_pick,
    in_blocks,
    in_cols,
    out_blocks,
    out_cols,
):
    tok = attn_out.shape[0]
    fsdp = lax.axis_size("fsdp")
    tensor = lax.axis_size("tensor")
    dps = lax.axis_size("dp")
    zs = fsdp // 2
    _, feats, shard = old_weights.shape
    n_out = fsdp * shard // HEAD
    n_in = tensor * feats // HEAD
    rows_all, k_in = in_cols.shape
    rows_out, k_out = out_cols.shape
    rows_in = rows_all // tensor
    pairs_in, pairs_out = rows_all * k_in, rows_out * k_out
    depth_k = depth_pick.shape[0]
    smem = pl.BlockSpec(memory_space=pltpu.SMEM)
    vmem = pl.BlockSpec(memory_space=pltpu.VMEM)
    dma = pltpu.SemaphoreType.DMA
    blocks = (n_out, tok, HEAD)
    scale = float(tok * dps * fsdp) ** (-0.5)

    n_sub = 4
    pairs = max(pairs_in, pairs_out)

    def stream_rows(rows):
        return -(-rows // (2 * dps * zs * 16)) * 16

    def stream_scratch(rows):
        u = stream_rows(rows)
        return [
            pltpu.VMEM((2 * dps * zs * u, HEAD), BF16),
            pltpu.VMEM((dps * zs, u, HEAD), BF16),
            pltpu.VMEM((dps * zs, u, HEAD), BF16),
            pltpu.VMEM((zs, u, HEAD), BF16),
            dma((dps, zs)),
            dma((dps, zs)),
            dma((dps, zs)),
            dma((dps, zs)),
            dma((zs,)),
            dma((zs,)),
            dma((2, dps, zs)),
            dma((zs,)),
            dma((dps, zs)),
        ]

    def stream_out(rows):
        return jax.ShapeDtypeStruct((2 * dps * zs * stream_rows(rows), HEAD), BF16)

    rows_o, rows_i = pairs_out * HEAD, rows_in * k_in * HEAD
    arrays = (
        attn_out,
        cotangent,
        old_weights,
        in_blocks.reshape(pairs_in, HEAD, HEAD),
        out_blocks.reshape(pairs_out, HEAD, HEAD),
    )
    grown, gattn, out_sum, in_sum = pl.pallas_call(
        functools.partial(
            kernel, (zs, dps, depth_k, k_in, k_out, rows_all, rows_out, pairs, n_sub)
        ),
        out_shape=(
            jax.ShapeDtypeStruct((tok, rows_out * HEAD), BF16),
            jax.ShapeDtypeStruct((tok, rows_in * HEAD), BF16),
            stream_out(rows_o),
            stream_out(rows_i),
        ),
        in_specs=[smem] * 2 + [pl.BlockSpec(memory_space=pl.ANY)] * 5,
        out_specs=(vmem, vmem, vmem, vmem),
        scratch_shapes=[
            pltpu.VMEM(attn_out.shape, BF16),
            pltpu.VMEM(cotangent.shape, BF16),
            pltpu.VMEM((old_weights.shape[0], feats // 2, shard), BF16),
            pltpu.VMEM((old_weights.shape[0], feats // 2, shard), BF16),
            pltpu.VMEM(arrays[3].shape, BF16),
            pltpu.VMEM(arrays[4].shape, BF16),
            dma((6,)),
            pltpu.VMEM((fsdp, feats, shard), BF16),
            pltpu.VMEM((pairs + 1, tok, HEAD), F32),
            pltpu.VMEM(blocks, BF16),
            pltpu.VMEM(blocks, BF16),
            pltpu.VMEM(blocks, BF16),
            pltpu.VMEM(blocks, BF16),
            pltpu.VMEM(blocks, BF16),
            pltpu.VMEM((tok, feats), BF16),
            pltpu.VMEM((tok, feats), F32),
            pltpu.VMEM((n_in, tok, HEAD), BF16),
            dma((fsdp, 2, n_sub, 4)),
            dma((fsdp, 2, n_sub)),
            dma((fsdp,)),
            dma((fsdp,)),
            dma((fsdp,)),
            dma((fsdp,)),
            dma,
            dma,
            *stream_scratch(rows_o),
            *stream_scratch(rows_i),
        ],
        compiler_params=pltpu.CompilerParams(
            collective_id=0, has_side_effects=True, vmem_limit_bytes=52 * 2**20
        ),
    )(
        index_table(depth_pick, in_cols, out_cols, max(n_in, n_out)),
        depth_coef,
        *arrays,
    )
    in_sum = in_sum[:rows_i].reshape(rows_in, k_in, HEAD, HEAD).astype(F32) * scale
    out_sum = out_sum[:rows_o].reshape(rows_out, k_out, HEAD, HEAD).astype(F32) * scale
    return grown, gattn, in_sum, out_sum


def solution(mesh):
    placed = (
        P(("dp", "fsdp"), None),
        P(("dp", "fsdp"), "tensor"),
        P(None, "tensor", "fsdp"),
        P(),
        P(),
        P(),
        P(),
        P("tensor", None, None, None),
        P("tensor", None),
    )
    return jax.shard_map(
        local,
        mesh=mesh,
        in_specs=placed,
        out_specs=(
            P(("dp", "fsdp"), "tensor"),
            P(("dp", "fsdp"), "tensor"),
            P("tensor", None, None, None),
            P("tensor", None, None, None),
        ),
        check_vma=False,
    )
```

```python
import functools

import jax
import jax.numpy as jnp
from jax import lax
from jax.experimental import pallas as pl
from jax.experimental.pallas import tpu as pltpu
from jax.sharding import PartitionSpec as P

HEAD = 128
MESH = pl.DeviceIdType.MESH
F32 = jnp.float32
BF16 = jnp.bfloat16


def dot(a, b, ca=1, cb=0):
    return lax.dot_general(a, b, (((ca,), (cb,)), ((), ())), preferred_element_type=F32)


def kernel(
    dims,
    table,
    coef,
    attn_hbm,
    cot_hbm,
    old_w_hbm,
    in_b_hbm,
    out_b_hbm,
    grown,
    gattn,
    out_full,
    in_full,
    attn,
    cot,
    old_w_first,
    old_w_last,
    in_b,
    out_b,
    load_sem,
    w_all,
    sums,
    og_mine,
    og_theirs,
    p_mine,
    p_theirs,
    oo,
    hid,
    hg_acc,
    hg_all,
    w_send,
    w_recv,
    og_send,
    og_recv,
    p_send,
    p_recv,
    hg_send,
    hg_recv,
    *streams,
):
    zs, dps, depth_k, k_in, k_out, rows_all, rows_out, pairs, n_sub = dims
    streams = (streams[:13], streams[13:])
    shard = w_all.shape[2]
    feats = w_all.shape[1]
    half_rows = feats // 2
    nb = shard // HEAD
    nl = feats // HEAD
    n_out = og_mine.shape[0]
    sub_rows = half_rows // n_sub
    pairs_in = rows_all * k_in
    pairs_out = rows_out * k_out
    targets = (table.shape[0] - depth_k) // 2 - 2 * pairs

    def in_col(r, k):
        return table[depth_k + k * rows_all + r]

    def out_col(r, k):
        return table[depth_k + pairs + k * rows_out + r]

    def in_link(i):
        return table[depth_k + 2 * pairs + i]

    def out_link(i):
        return table[depth_k + 3 * pairs + targets + i]

    def load(i, src, dst):
        return pltpu.make_async_copy(src, dst, load_sem.at[i])

    def load_mix(half, i, dst):
        part = pl.ds(pl.multiple_of(half * half_rows, half_rows), half_rows)
        return load(i, old_w_hbm.at[:, part], dst)

    others = [
        load(2, cot_hbm, cot),
        load(3, out_b_hbm, out_b),
        load(4, attn_hbm, attn),
        load(5, in_b_hbm, in_b),
    ]
    rows_in = gattn.shape[1] // HEAD

    dp = lax.axis_index("dp")
    fs = lax.axis_index("fsdp")
    tn = lax.axis_index("tensor")
    z = fs // 2
    core = fs % 2
    h = dp % 2
    o = 1 - h
    other_core = {"fsdp": 2 * z + 1 - core}
    other_dp = {"dp": dp + 1 - 2 * h}
    other_tn = {"tensor": 1 - tn}
    above = {"fsdp": fs + 2}
    below = {"fsdp": fs - 2}

    load_first = load_mix(h, 0, old_w_first)
    load_last = load_mix(o, 1, old_w_last)
    load_first.start()
    load_last.start()
    for one_load in others:
        one_load.start()

    def w_copy(f, half, sub, kind, to):
        start = pl.multiple_of(half * half_rows + sub * sub_rows, sub_rows)
        piece = w_all.at[f, pl.ds(start, sub_rows)]
        return pltpu.make_async_remote_copy(
            src_ref=piece,
            dst_ref=piece,
            send_sem=w_send.at[f, half, sub, kind],
            recv_sem=w_recv.at[f, half, sub],
            device_id=to,
            device_id_type=MESH,
        )

    def chunk_copy(src, dst, send, recv, f):
        part = pl.ds(f * nb, nb)
        return pltpu.make_async_remote_copy(
            src_ref=src.at[part],
            dst_ref=dst.at[part],
            send_sem=send.at[f],
            recv_sem=recv.at[f],
            device_id=other_tn,
            device_id_type=MESH,
        )

    def hg_copy(half):
        part = hg_all.at[pl.ds(half * nl, nl)]
        return pltpu.make_async_remote_copy(
            src_ref=part,
            dst_ref=part,
            send_sem=hg_send,
            recv_sem=hg_recv,
            device_id=other_tn,
            device_id_type=MESH,
        )

    barrier = pltpu.get_barrier_semaphore()
    for to in (other_core, other_tn):
        pl.semaphore_signal(barrier, inc=1, device_id=to, device_id_type=MESH)
    for i in range(1, dps):
        to = {"dp": (dp + i) % dps}
        pl.semaphore_signal(barrier, inc=1, device_id=to, device_id_type=MESH)
    for i in range(1, zs):
        to = {"fsdp": 2 * ((z + i) % zs) + core}
        pl.semaphore_signal(barrier, inc=1, device_id=to, device_id_type=MESH)
    pl.semaphore_wait(barrier, dps + zs)

    mix_rows = 64

    def mix(half, old_w, sub):
        def body(i, _):
            start = sub * sub_rows + i * mix_rows
            part = pl.ds(pl.multiple_of(start, mix_rows), mix_rows)
            to = pl.ds(pl.multiple_of(half * half_rows + start, mix_rows), mix_rows)
            total = coef[0] * old_w[table[0], part, :].astype(F32)
            for j in range(1, depth_k):
                total = total + coef[j] * old_w[table[j], part, :].astype(F32)
            w_all[fs, to, :] = total.astype(BF16)
            return 0

        lax.fori_loop(0, sub_rows // mix_rows, body, 0)

    load_first.wait()

    def first_half(q, _):
        mix(h, old_w_first, q)

        @pl.when(z < zs - 1)
        def _():
            w_copy(fs, h, q, 0, above).start()

        @pl.when(z > 0)
        def _():
            w_copy(fs, h, q, 1, below).start()

        w_copy(fs, h, q, 3, other_core).start()
        return 0

    lax.fori_loop(0, n_sub, first_half, 0)
    load_last.wait()

    def second_half(q, _):
        mix(o, old_w_last, q)
        w_copy(fs, o, q, 3, other_core).start()
        return 0

    lax.fori_loop(0, n_sub, second_half, 0)
    others[0].wait()
    others[1].wait()

    sums[pairs] = jnp.zeros((HEAD, HEAD), F32)

    def back_row(r, _):
        cols = pl.ds(pl.multiple_of(r * HEAD, HEAD), HEAD)
        for k in range(k_out):
            j = r * k_out + k
            sums[j] = dot(cot[:, cols], out_b[j], 1, 1) + sums[out_link(k * rows_out + r)]
        return 0

    lax.fori_loop(0, rows_out, back_row, 0, unroll=4)

    def back_block(b, _):
        og_mine[b] = sums[out_link(pairs + b)].astype(BF16)
        return 0

    lax.fori_loop(0, n_out, back_block, 0, unroll=4)

    def shard_of(s, i, body):
        zz = z - s + 2 * s * (i // 2)
        cc = (core + i) % 2
        live = (zz >= 0) & (zz < zs) & ((s > 0) | (i < 2))

        @pl.when(live)
        def _():
            body(zz * 2 + cc, i % 2)

    def over_shards(s, body):
        def one(i, _):
            shard_of(s, i, body)
            return 0

        lax.fori_loop(0, 4, one, 0)

    def og_start(s, _):
        over_shards(s, lambda f, mine: chunk_copy(og_mine, og_theirs, og_send, og_recv, f).start())
        return 0

    lax.fori_loop(0, zs, og_start, 0)

    def relay(s, q):
        for way in range(2):
            zz = z - s + 2 * s * way
            nxt = z + 1 - 2 * way
            f = 2 * zz + core

            @pl.when((zz >= 0) & (zz < zs))
            def _():
                w_copy(f, h, q, way, other_dp).wait_recv()

                @pl.when((nxt >= 0) & (nxt < zs))
                def _():
                    w_copy(f, h, q, way, above if way == 0 else below).start()

                w_copy(f, h, q, 2, other_dp).start()
                w_copy(f, h, q, 3, other_core).start()

    for q in range(n_sub // 2):
        relay(1, q)

    others[2].wait()
    others[3].wait()

    def hid_row(r, _):
        cols = pl.ds(pl.multiple_of(r * HEAD, HEAD), HEAD)
        for k in range(k_in):
            j = r * k_in + k
            sums[j] = dot(attn[:, cols], in_b[j]) + sums[in_link(k * rows_all + r)]
        return 0

    lax.fori_loop(0, rows_all, hid_row, 0, unroll=4)
    for b in range(nl):
        hid[:, b * HEAD : (b + 1) * HEAD] = sums[in_link(pairs + tn * nl + b)].astype(BF16)

    for q in range(n_sub // 2, n_sub):
        relay(1, q)

    hg_acc[...] = jnp.zeros_like(hg_acc)

    def forward(f):
        part = dot(hid[...], w_all[f]).astype(BF16)
        for b in range(nb):
            p_mine[f * nb + b] = part[:, b * HEAD : (b + 1) * HEAD]
        chunk_copy(p_mine, p_theirs, p_send, p_recv, f).start()

    def backward(f, flip):
        chunk_copy(og_mine, og_theirs, og_send, og_recv, f).wait_recv()
        blocks = [
            (og_mine[f * nb + b].astype(F32) + og_theirs[f * nb + b].astype(F32)).astype(BF16)
            for b in range(nb)
        ]
        hg_acc[...] += dot(w_all[f], jnp.concatenate(blocks, axis=1), 1, 1)

    def first(f, flip):
        @pl.when(flip == 1)
        def _():
            def came(q, _):
                w_copy(f, 0, q, 3, other_core).wait_recv()
                w_copy(f, 1, q, 3, other_core).wait_recv()
                return 0

            lax.fori_loop(0, n_sub, came, 0)

        forward(f)

    def pass_on(s, q):
        for way in range(2):
            zz = z - s + 2 * s * way
            f = 2 * zz + core

            @pl.when((zz >= 0) & (zz < zs) & (s > 0))
            def _():
                w_copy(f, o, q, 2, other_dp).wait_recv()
                w_copy(f, o, q, 3, other_core).start()

    def step(s, _):
        def part(q, _):
            @pl.when(s >= 2)
            def _():
                relay(s, q)

            pass_on(s - (q == 0).astype(jnp.int32), (q + n_sub - 1) % n_sub)
            shard_of(s - 1, q, first)

            @pl.when((s >= 2) & (s < zs))
            def _():
                shard_of(s - 1, q, backward)

            @pl.when(s == 2)
            def _():
                shard_of(0, q, backward)

            return 0

        lax.fori_loop(0, n_sub, part, 0)
        return 0

    lax.fori_loop(1, zs + 1, step, 0)
    over_shards(zs - 1, backward)

    for b in range(nl):
        hg_all[tn * nl + b] = hg_acc[b * HEAD : (b + 1) * HEAD, :].T.astype(BF16)
    hg_copy(tn).start()

    def piece_copy(src, dst, send, recv, to):
        return pltpu.make_async_remote_copy(
            src_ref=src, dst_ref=dst, send_sem=send, recv_sem=recv, device_id=to, device_id_type=MESH
        )

    class Stream:
        def __init__(self, refs, full):
            (self.g, self.from_core, self.from_dp, self.from_z) = refs[:4]
            (self.c_s, self.c_r, self.y_s, self.y_r, self.z_s, self.z_r) = refs[4:10]
            (self.a_r, self.az_s, self.ay_s) = refs[10:13]
            self.full = full
            self.u = self.from_z.shape[1]

        def rows(self, c, e, q):
            return pl.ds(pl.multiple_of(((c * dps + e) * zs + q) * self.u, self.u), self.u)

        def core_copy(self, e, q):
            return piece_copy(
                self.g.at[self.rows(1 - core, e, q)],
                self.from_core.at[e * zs + q],
                self.c_s.at[e, q],
                self.c_r.at[e, q],
                other_core,
            )

        def dp_copy(self, src, e, q):
            return piece_copy(
                self.g.at[self.rows(core, e, q)],
                self.from_dp.at[src * zs + q],
                self.y_s.at[e, q],
                self.y_r.at[src, q],
                {"dp": e},
            )

        def z_copy(self, src, q):
            return piece_copy(
                self.g.at[self.rows(core, dp, q)],
                self.from_z.at[src],
                self.z_s.at[q],
                self.z_r.at[src],
                {"fsdp": 2 * q + core},
            )

        def full_copy(self, c, e, q, send, to):
            piece = self.full.at[self.rows(c, e, q)]
            return piece_copy(piece, piece, send, self.a_r.at[c, e, q], to)

        def gather_z(self, q):
            return self.full_copy(core, dp, z, self.az_s.at[q], {"fsdp": 2 * q + core})

        def gather_dp(self, e, q):
            return self.full_copy(core, dp, q, self.ay_s.at[e, q], {"dp": e})

        def gather_core(self, e, q):
            return self.full_copy(core, e, q, self.c_s.at[e, q], other_core)

        def came(self, c, e, q):
            self.full_copy(c, e, q, self.c_s.at[e, q], other_core).wait_recv()

        def each_q(self, body):
            def one(i, _):
                body((z + 1 + i) % zs)
                return 0

            lax.fori_loop(0, zs, one, 0)

        def each_e(self, body, own=False):
            def one(i, _):
                body((dp + 1 + i) % dps)
                return 0

            lax.fori_loop(0, dps if own else dps - 1, one, 0)

        def start_core(self):
            self.each_e(lambda e: self.each_q(lambda q: self.core_copy(e, q).start()), True)

        def core_sums(self):
            def one(e, q):
                self.core_copy(e, q).wait()
                rows = self.rows(core, e, q)
                total = self.g[rows, :].astype(F32) + self.from_core[e * zs + q].astype(F32)
                self.g[rows, :] = total.astype(BF16)

                @pl.when(e != dp)
                def _():
                    self.dp_copy(dp, e, q).start()

            self.each_e(lambda e: self.each_q(lambda q: one(e, q)), True)

        def dp_sums(self, rows_between, row):
            each = -(-rows_between // zs)

            def one(q):
                for i in range(each):
                    r = q * each + i

                    @pl.when(r < rows_between)
                    def _():
                        row(r)

                rows = self.rows(core, dp, q)
                total = self.g[rows, :].astype(F32)
                for i in range(1, dps):
                    src = (dp + i) % dps
                    self.dp_copy(src, dp, q).wait_recv()
                    total = total + self.from_dp[src * zs + q].astype(F32)
                self.g[rows, :] = total.astype(BF16)

                @pl.when(q != z)
                def _():
                    self.z_copy(z, q).start()

            self.each_q(one)

        def z_sums(self):
            total = self.g[self.rows(core, dp, z), :].astype(F32)
            for i in range(1, zs):
                src = (z + i) % zs
                self.z_copy(src, z).wait_recv()
                total = total + self.from_z[src].astype(F32)
            self.full[self.rows(core, dp, z), :] = total.astype(BF16)

            def to_z(i, _):
                self.gather_z((z + i) % zs).start()
                return 0

            lax.fori_loop(1, zs, to_z, 0)
            self.each_e(lambda e: self.gather_dp(e, z).start())
            self.gather_core(dp, z).start()

        def near(self, body):
            def one(s, _):
                for zz in (z - s, z + s):
                    @pl.when((zz >= 0) & (zz < zs))
                    def _():
                        body(zz)

                return 0

            lax.fori_loop(1, zs, one, 0)

        def forward_z(self):
            def one(q):
                self.came(core, dp, q)
                self.each_e(lambda e: self.gather_dp(e, q).start())
                self.gather_core(dp, q).start()

            self.near(one)

        def forward_dp(self):
            def one(q):
                def each(e):
                    self.came(core, e, q)
                    self.gather_core(e, q).start()

                self.each_e(each)

            one(z)
            self.near(one)

        def finish(self):
            self.each_e(lambda e: self.each_q(lambda q: self.came(1 - core, e, q)), True)

        def drain(self):
            self.each_e(lambda e: self.each_q(lambda q: self.dp_copy(dp, e, q).wait_send()))
            self.each_e(lambda e: self.each_q(lambda q: self.gather_dp(e, q).wait_send()))
            self.each_e(lambda e: self.each_q(lambda q: self.gather_core(e, q).wait_send()), True)

            def to_z(i, _):
                self.z_copy(z, (z + i) % zs).wait_send()
                self.gather_z((z + i) % zs).wait_send()
                return 0

            lax.fori_loop(1, zs, to_z, 0)

        def clear_tail(self, used):
            spare = self.g.shape[0] - used
            if spare > 0:
                self.g[used:, :] = jnp.zeros((spare, HEAD), BF16)

    outs, ins = Stream(streams[0], out_full), Stream(streams[1], in_full)
    outs.clear_tail(pairs_out * HEAD)
    ins.clear_tail(rows_in * k_in * HEAD)

    def add_shard(f, _):
        chunk_copy(p_mine, p_theirs, p_send, p_recv, f).wait_recv()
        for b in range(nb):
            oo[f * nb + b] = (
                p_mine[f * nb + b].astype(F32) + p_theirs[f * nb + b].astype(F32)
            ).astype(BF16)
        return 0

    lax.fori_loop(0, 2 * zs, add_shard, 0)

    def out_row(r, _):
        cols = pl.ds(pl.multiple_of(r * HEAD, HEAD), HEAD)
        for k in range(k_out):
            j = r * k_out + k
            to = pl.ds(pl.multiple_of(j * HEAD, HEAD), HEAD)
            outs.g[to, :] = dot(oo[out_col(r, k)], cot[:, cols], 0, 0).astype(BF16)
        return 0

    lax.fori_loop(0, rows_out, out_row, 0, unroll=4)
    outs.start_core()
    hg_copy(1 - tn).wait_recv()

    def in_row(r, _):
        mine = tn * rows_in + r
        mine_cols = pl.ds(pl.multiple_of(mine * HEAD, HEAD), HEAD)
        for k in range(k_in):
            block = hg_all[in_col(mine, k)]
            to = pl.ds(pl.multiple_of((r * k_in + k) * HEAD, HEAD), HEAD)
            ins.g[to, :] = dot(attn[:, mine_cols], block, 0, 0).astype(BF16)
        return 0

    lax.fori_loop(0, rows_in, in_row, 0, unroll=2)
    ins.start_core()
    outs.core_sums()
    ins.core_sums()

    def grown_row(r):
        cols = pl.ds(pl.multiple_of(r * HEAD, HEAD), HEAD)
        total = None
        for k in range(k_out):
            term = dot(oo[out_col(r, k)], out_b[r * k_out + k])
            total = term if total is None else total + term
        grown[:, cols] = total.astype(BF16)

    def gattn_row(r):
        cols = pl.ds(pl.multiple_of(r * HEAD, HEAD), HEAD)
        mine = tn * rows_in + r
        total = None
        for k in range(k_in):
            term = dot(hg_all[in_col(mine, k)], in_b[mine * k_in + k], 1, 1)
            total = term if total is None else total + term
        gattn[:, cols] = total.astype(BF16)

    outs.dp_sums(rows_out, grown_row)
    ins.dp_sums(rows_in, gattn_row)
    outs.z_sums()
    ins.z_sums()
    outs.forward_z()
    ins.forward_z()
    outs.forward_dp()
    ins.forward_dp()
    outs.finish()
    ins.finish()
    outs.drain()
    ins.drain()

    def send_done(f, _):
        chunk_copy(og_mine, og_theirs, og_send, og_recv, f).wait_send()
        chunk_copy(p_mine, p_theirs, p_send, p_recv, f).wait_send()
        return 0

    lax.fori_loop(0, 2 * zs, send_done, 0)
    hg_copy(tn).wait_send()

    def own_done(q, _):
        @pl.when(z < zs - 1)
        def _():
            w_copy(fs, h, q, 0, above).wait_send()

        @pl.when(z > 0)
        def _():
            w_copy(fs, h, q, 1, below).wait_send()

        w_copy(fs, h, q, 3, other_core).wait_send()
        w_copy(fs, o, q, 3, other_core).wait_send()
        return 0

    lax.fori_loop(0, n_sub, own_done, 0)

    def relay_done(i, _):
        s = 1 + i // n_sub
        q = i % n_sub
        for way in range(2):
            zz = z - s + 2 * s * way
            nxt = z + 1 - 2 * way
            f = 2 * zz + core

            @pl.when((zz >= 0) & (zz < zs))
            def _():
                @pl.when((nxt >= 0) & (nxt < zs))
                def _():
                    w_copy(f, h, q, way, above if way == 0 else below).wait_send()

                w_copy(f, h, q, 2, other_dp).wait_send()
                w_copy(f, h, q, 3, other_core).wait_send()
                w_copy(f, o, q, 3, other_core).wait_send()

        return 0

    lax.fori_loop(0, (zs - 1) * n_sub, relay_done, 0)


def finish_kernel(
    scale, grown_in, gattn_in, out_in, in_in, grown, gattn, out_sum, in_sum, out_buf, in_buf, sems
):
    copies = [
        pltpu.make_async_copy(grown_in, grown, sems.at[0]),
        pltpu.make_async_copy(gattn_in, gattn, sems.at[1]),
    ]
    for one in copies:
        one.start()
    spot = 2
    for src, buf, dst, parts in ((out_in, out_buf, out_sum, 4), (in_in, in_buf, in_sum, 2)):
        blocks = buf.shape[0]
        for i in range(parts):
            lo, hi = blocks * i // parts, blocks * (i + 1) // parts

            def block(b, _):
                rows = pl.ds(pl.multiple_of(b * HEAD, HEAD), HEAD)
                buf[b] = src[rows, :].astype(F32) * scale
                return 0

            lax.fori_loop(lo, hi, block, 0)
            part = pl.ds(lo, hi - lo)
            copies.append(pltpu.make_async_copy(buf.at[part], dst.at[part], sems.at[spot]))
            copies[-1].start()
            spot += 1
    for one in copies:
        one.wait()


def index_table(pick, in_cols, out_cols, targets):
    pairs = max(in_cols.size, out_cols.size)
    flats, orders = [], []
    for cols in (in_cols, out_cols):
        rows, terms = cols.shape
        short = (0, pairs - cols.size)
        order = jnp.arange(rows, dtype=jnp.int32)[None, :] * terms
        order = order + jnp.arange(terms, dtype=jnp.int32)[:, None]
        flats.append(jnp.pad(cols.T.reshape(-1), short, constant_values=-1))
        orders.append(jnp.pad(order.reshape(-1), short, constant_values=pairs))
    flat, order = jnp.stack(flats), jnp.stack(orders)
    named = jnp.broadcast_to(jnp.arange(targets, dtype=jnp.int32), (2, targets))
    want = jnp.concatenate([flat, named], axis=1)
    limit = jnp.concatenate([order, jnp.full((2, targets), pairs, jnp.int32)], axis=1)
    same = (want[:, :, None] == flat[:, None, :]) & (order[:, None, :] < limit[:, :, None])
    found = jnp.max(jnp.where(same, order[:, None, :], -1), axis=2)
    found = jnp.where(found < 0, pairs, found)
    return jnp.concatenate([pick, flat.reshape(-1), found.reshape(-1)])


def local(
    attn_out,
    cotangent,
    old_weights,
    depth_coef,
    depth_pick,
    in_blocks,
    in_cols,
    out_blocks,
    out_cols,
):
    tok = attn_out.shape[0]
    fsdp = lax.axis_size("fsdp")
    tensor = lax.axis_size("tensor")
    dps = lax.axis_size("dp")
    zs = fsdp // 2
    _, feats, shard = old_weights.shape
    n_out = fsdp * shard // HEAD
    n_in = tensor * feats // HEAD
    rows_all, k_in = in_cols.shape
    rows_out, k_out = out_cols.shape
    rows_in = rows_all // tensor
    pairs_in, pairs_out = rows_all * k_in, rows_out * k_out
    depth_k = depth_pick.shape[0]
    smem = pl.BlockSpec(memory_space=pltpu.SMEM)
    vmem = pl.BlockSpec(memory_space=pltpu.VMEM)
    dma = pltpu.SemaphoreType.DMA
    blocks = (n_out, tok, HEAD)
    scale = float(tok * dps * fsdp) ** (-0.5)

    n_sub = 4
    pairs = max(pairs_in, pairs_out)

    def stream_rows(rows):
        return -(-rows // (2 * dps * zs * 16)) * 16

    def stream_scratch(rows):
        u = stream_rows(rows)
        return [
            pltpu.VMEM((2 * dps * zs * u, HEAD), BF16),
            pltpu.VMEM((dps * zs, u, HEAD), BF16),
            pltpu.VMEM((dps * zs, u, HEAD), BF16),
            pltpu.VMEM((zs, u, HEAD), BF16),
            dma((dps, zs)),
            dma((dps, zs)),
            dma((dps, zs)),
            dma((dps, zs)),
            dma((zs,)),
            dma((zs,)),
            dma((2, dps, zs)),
            dma((zs,)),
            dma((dps, zs)),
        ]

    def stream_out(rows):
        return jax.ShapeDtypeStruct((2 * dps * zs * stream_rows(rows), HEAD), BF16)

    rows_o, rows_i = pairs_out * HEAD, rows_in * k_in * HEAD
    arrays = (
        attn_out,
        cotangent,
        old_weights,
        in_blocks.reshape(pairs_in, HEAD, HEAD),
        out_blocks.reshape(pairs_out, HEAD, HEAD),
    )
    grown, gattn, out_sum, in_sum = pl.pallas_call(
        functools.partial(
            kernel, (zs, dps, depth_k, k_in, k_out, rows_all, rows_out, pairs, n_sub)
        ),
        out_shape=(
            jax.ShapeDtypeStruct((tok, rows_out * HEAD), BF16),
            jax.ShapeDtypeStruct((tok, rows_in * HEAD), BF16),
            stream_out(rows_o),
            stream_out(rows_i),
        ),
        in_specs=[smem] * 2 + [pl.BlockSpec(memory_space=pl.ANY)] * 5,
        out_specs=(vmem, vmem, vmem, vmem),
        scratch_shapes=[
            pltpu.VMEM(attn_out.shape, BF16),
            pltpu.VMEM(cotangent.shape, BF16),
            pltpu.VMEM((old_weights.shape[0], feats // 2, shard), BF16),
            pltpu.VMEM((old_weights.shape[0], feats // 2, shard), BF16),
            pltpu.VMEM(arrays[3].shape, BF16),
            pltpu.VMEM(arrays[4].shape, BF16),
            dma((6,)),
            pltpu.VMEM((fsdp, feats, shard), BF16),
            pltpu.VMEM((pairs + 1, tok, HEAD), F32),
            pltpu.VMEM(blocks, BF16),
            pltpu.VMEM(blocks, BF16),
            pltpu.VMEM(blocks, BF16),
            pltpu.VMEM(blocks, BF16),
            pltpu.VMEM(blocks, BF16),
            pltpu.VMEM((tok, feats), BF16),
            pltpu.VMEM((feats, tok), F32),
            pltpu.VMEM((n_in, tok, HEAD), BF16),
            dma((fsdp, 2, n_sub, 4)),
            dma((fsdp, 2, n_sub)),
            dma((fsdp,)),
            dma((fsdp,)),
            dma((fsdp,)),
            dma((fsdp,)),
            dma,
            dma,
            *stream_scratch(rows_o),
            *stream_scratch(rows_i),
        ],
        compiler_params=pltpu.CompilerParams(
            collective_id=0, has_side_effects=True, vmem_limit_bytes=52 * 2**20
        ),
    )(
        index_table(depth_pick, in_cols, out_cols, max(n_in, n_out)),
        depth_coef,
        *arrays,
    )
    anywhere = pl.BlockSpec(memory_space=pl.ANY)
    out_blocks_shape = (pairs_out, HEAD, HEAD)
    in_blocks_shape = (rows_in * k_in, HEAD, HEAD)
    grown, gattn, out_sum, in_sum = pl.pallas_call(
        functools.partial(finish_kernel, scale),
        out_shape=(
            jax.ShapeDtypeStruct(grown.shape, BF16),
            jax.ShapeDtypeStruct(gattn.shape, BF16),
            jax.ShapeDtypeStruct(out_blocks_shape, F32),
            jax.ShapeDtypeStruct(in_blocks_shape, F32),
        ),
        in_specs=[anywhere, anywhere, vmem, vmem],
        out_specs=(anywhere,) * 4,
        scratch_shapes=[
            pltpu.VMEM(out_blocks_shape, F32),
            pltpu.VMEM(in_blocks_shape, F32),
            dma((8,)),
        ],
        compiler_params=pltpu.CompilerParams(vmem_limit_bytes=16 * 2**20),
    )(grown, gattn, out_sum, in_sum)
    in_sum = in_sum.reshape(rows_in, k_in, HEAD, HEAD)
    out_sum = out_sum.reshape(rows_out, k_out, HEAD, HEAD)
    return grown, gattn, in_sum, out_sum


def solution(mesh):
    placed = (
        P(("dp", "fsdp"), None),
        P(("dp", "fsdp"), "tensor"),
        P(None, "tensor", "fsdp"),
        P(),
        P(),
        P(),
        P(),
        P("tensor", None, None, None),
        P("tensor", None),
    )
    return jax.shard_map(
        local,
        mesh=mesh,
        in_specs=placed,
        out_specs=(
            P(("dp", "fsdp"), "tensor"),
            P(("dp", "fsdp"), "tensor"),
            P("tensor", None, None, None),
            P("tensor", None, None, None),
        ),
        check_vma=False,
    )
```

```python
import functools

import jax
import jax.numpy as jnp
from jax import lax
from jax.experimental import pallas as pl
from jax.experimental.pallas import tpu as pltpu
from jax.sharding import PartitionSpec as P

HEAD = 128
MESH = pl.DeviceIdType.MESH
F32 = jnp.float32
BF16 = jnp.bfloat16


def dot(a, b, ca=1, cb=0):
    return lax.dot_general(a, b, (((ca,), (cb,)), ((), ())), preferred_element_type=F32)


def kernel(
    dims,
    table,
    coef,
    attn_hbm,
    cot_hbm,
    old_w_hbm,
    in_b_hbm,
    out_b_hbm,
    grown,
    gattn,
    out_full,
    in_full,
    attn,
    cot,
    old_w_first,
    old_w_last,
    in_b,
    out_b,
    load_sem,
    w_all,
    sums,
    og_mine,
    og_theirs,
    p_mine,
    p_theirs,
    oo,
    hid,
    hg_acc,
    hg_all,
    w_send,
    w_recv,
    og_send,
    og_recv,
    p_send,
    p_recv,
    hg_send,
    hg_recv,
    *streams,
):
    zs, dps, depth_k, k_in, k_out, rows_all, rows_out, pairs, n_sub = dims
    streams = (streams[:13], streams[13:])
    shard = w_all.shape[2]
    feats = w_all.shape[1]
    half_rows = feats // 2
    nb = shard // HEAD
    nl = feats // HEAD
    n_out = og_mine.shape[0]
    sub_rows = half_rows // n_sub
    pairs_in = rows_all * k_in
    pairs_out = rows_out * k_out
    targets = (table.shape[0] - depth_k) // 2 - 2 * pairs

    def in_col(r, k):
        return table[depth_k + k * rows_all + r]

    def out_col(r, k):
        return table[depth_k + pairs + k * rows_out + r]

    def in_link(i):
        return table[depth_k + 2 * pairs + i]

    def out_link(i):
        return table[depth_k + 3 * pairs + targets + i]

    def load(i, src, dst):
        return pltpu.make_async_copy(src, dst, load_sem.at[i])

    def load_mix(half, i, dst):
        part = pl.ds(pl.multiple_of(half * half_rows, half_rows), half_rows)
        return load(i, old_w_hbm.at[:, part], dst)

    others = [
        load(2, cot_hbm, cot),
        load(3, out_b_hbm, out_b),
        load(4, attn_hbm, attn),
        load(5, in_b_hbm, in_b),
    ]
    rows_in = gattn.shape[1] // HEAD

    dp = lax.axis_index("dp")
    fs = lax.axis_index("fsdp")
    tn = lax.axis_index("tensor")
    z = fs // 2
    core = fs % 2
    h = dp % 2
    o = 1 - h
    other_core = {"fsdp": 2 * z + 1 - core}
    other_dp = {"dp": dp + 1 - 2 * h}
    other_tn = {"tensor": 1 - tn}
    above = {"fsdp": fs + 2}
    below = {"fsdp": fs - 2}

    load_first = load_mix(h, 0, old_w_first)
    load_last = load_mix(o, 1, old_w_last)
    load_first.start()
    load_last.start()
    for one_load in others:
        one_load.start()

    def w_copy(f, half, sub, kind, to):
        start = pl.multiple_of(half * half_rows + sub * sub_rows, sub_rows)
        piece = w_all.at[f, pl.ds(start, sub_rows)]
        return pltpu.make_async_remote_copy(
            src_ref=piece,
            dst_ref=piece,
            send_sem=w_send.at[f, half, sub, kind],
            recv_sem=w_recv.at[f, half, sub],
            device_id=to,
            device_id_type=MESH,
        )

    def chunk_copy(src, dst, send, recv, f):
        part = pl.ds(f * nb, nb)
        return pltpu.make_async_remote_copy(
            src_ref=src.at[part],
            dst_ref=dst.at[part],
            send_sem=send.at[f],
            recv_sem=recv.at[f],
            device_id=other_tn,
            device_id_type=MESH,
        )

    def hg_copy(half):
        part = hg_all.at[pl.ds(half * nl, nl)]
        return pltpu.make_async_remote_copy(
            src_ref=part,
            dst_ref=part,
            send_sem=hg_send,
            recv_sem=hg_recv,
            device_id=other_tn,
            device_id_type=MESH,
        )

    barrier = pltpu.get_barrier_semaphore()
    for to in (other_core, other_tn):
        pl.semaphore_signal(barrier, inc=1, device_id=to, device_id_type=MESH)
    for i in range(1, dps):
        to = {"dp": (dp + i) % dps}
        pl.semaphore_signal(barrier, inc=1, device_id=to, device_id_type=MESH)
    for i in range(1, zs):
        to = {"fsdp": 2 * ((z + i) % zs) + core}
        pl.semaphore_signal(barrier, inc=1, device_id=to, device_id_type=MESH)
    pl.semaphore_wait(barrier, dps + zs)

    mix_rows = 64

    def mix(half, old_w, sub):
        def body(i, _):
            start = sub * sub_rows + i * mix_rows
            part = pl.ds(pl.multiple_of(start, mix_rows), mix_rows)
            to = pl.ds(pl.multiple_of(half * half_rows + start, mix_rows), mix_rows)
            total = coef[0] * old_w[table[0], part, :].astype(F32)
            for j in range(1, depth_k):
                total = total + coef[j] * old_w[table[j], part, :].astype(F32)
            w_all[fs, to, :] = total.astype(BF16)
            return 0

        lax.fori_loop(0, sub_rows // mix_rows, body, 0)

    load_first.wait()

    def first_half(q, _):
        mix(h, old_w_first, q)

        @pl.when(z < zs - 1)
        def _():
            w_copy(fs, h, q, 0, above).start()

        @pl.when(z > 0)
        def _():
            w_copy(fs, h, q, 1, below).start()

        w_copy(fs, h, q, 3, other_core).start()
        return 0

    lax.fori_loop(0, n_sub, first_half, 0)
    load_last.wait()

    def second_half(q, _):
        mix(o, old_w_last, q)
        w_copy(fs, o, q, 3, other_core).start()
        return 0

    lax.fori_loop(0, n_sub, second_half, 0)
    others[0].wait()
    others[1].wait()

    sums[pairs] = jnp.zeros((HEAD, HEAD), F32)

    def back_row(r, _):
        cols = pl.ds(pl.multiple_of(r * HEAD, HEAD), HEAD)
        for k in range(k_out):
            j = r * k_out + k
            sums[j] = dot(cot[:, cols], out_b[j], 1, 1) + sums[out_link(k * rows_out + r)]
        return 0

    lax.fori_loop(0, rows_out, back_row, 0, unroll=4)

    def back_block(b, _):
        og_mine[b] = sums[out_link(pairs + b)].astype(BF16)
        return 0

    lax.fori_loop(0, n_out, back_block, 0, unroll=4)

    def shard_of(s, i, body):
        zz = z - s + 2 * s * (i // 2)
        cc = (core + i) % 2
        live = (zz >= 0) & (zz < zs) & ((s > 0) | (i < 2))

        @pl.when(live)
        def _():
            body(zz * 2 + cc, i % 2)

    def over_shards(s, body):
        def one(i, _):
            shard_of(s, i, body)
            return 0

        lax.fori_loop(0, 4, one, 0)

    def og_start(s, _):
        over_shards(s, lambda f, mine: chunk_copy(og_mine, og_theirs, og_send, og_recv, f).start())
        return 0

    lax.fori_loop(0, zs, og_start, 0)

    def relay(s, q):
        for way in range(2):
            zz = z - s + 2 * s * way
            nxt = z + 1 - 2 * way
            f = 2 * zz + core

            @pl.when((zz >= 0) & (zz < zs))
            def _():
                w_copy(f, h, q, way, other_dp).wait_recv()

                @pl.when((nxt >= 0) & (nxt < zs))
                def _():
                    w_copy(f, h, q, way, above if way == 0 else below).start()

                w_copy(f, h, q, 2, other_dp).start()
                w_copy(f, h, q, 3, other_core).start()

    for q in range(n_sub // 2):
        relay(1, q)

    others[2].wait()
    others[3].wait()

    def hid_row(r, _):
        cols = pl.ds(pl.multiple_of(r * HEAD, HEAD), HEAD)
        for k in range(k_in):
            j = r * k_in + k
            sums[j] = dot(attn[:, cols], in_b[j]) + sums[in_link(k * rows_all + r)]
        return 0

    lax.fori_loop(0, rows_all, hid_row, 0, unroll=4)
    for b in range(nl):
        hid[:, b * HEAD : (b + 1) * HEAD] = sums[in_link(pairs + tn * nl + b)].astype(BF16)

    for q in range(n_sub // 2, n_sub):
        relay(1, q)

    hg_acc[...] = jnp.zeros_like(hg_acc)

    def forward(f):
        part = dot(hid[...], w_all[f]).astype(BF16)
        for b in range(nb):
            p_mine[f * nb + b] = part[:, b * HEAD : (b + 1) * HEAD]
        chunk_copy(p_mine, p_theirs, p_send, p_recv, f).start()

    def backward(f, flip):
        chunk_copy(og_mine, og_theirs, og_send, og_recv, f).wait_recv()
        blocks = [
            (og_mine[f * nb + b].astype(F32) + og_theirs[f * nb + b].astype(F32)).astype(BF16)
            for b in range(nb)
        ]
        hg_acc[...] += dot(w_all[f], jnp.concatenate(blocks, axis=1), 1, 1)

    def first(f, flip):
        @pl.when(flip == 1)
        def _():
            def came(q, _):
                w_copy(f, 0, q, 3, other_core).wait_recv()
                w_copy(f, 1, q, 3, other_core).wait_recv()
                return 0

            lax.fori_loop(0, n_sub, came, 0)

        forward(f)

    def pass_on(s, q):
        for way in range(2):
            zz = z - s + 2 * s * way
            f = 2 * zz + core

            @pl.when((zz >= 0) & (zz < zs) & (s > 0))
            def _():
                w_copy(f, o, q, 2, other_dp).wait_recv()
                w_copy(f, o, q, 3, other_core).start()

    def step(s, _):
        def part(q, _):
            @pl.when(s >= 2)
            def _():
                relay(s, q)

            pass_on(s - (q == 0).astype(jnp.int32), (q + n_sub - 1) % n_sub)
            shard_of(s - 1, q, first)

            @pl.when((s >= 2) & (s < zs))
            def _():
                shard_of(s - 1, q, backward)

            @pl.when(s == 2)
            def _():
                shard_of(0, q, backward)

            return 0

        lax.fori_loop(0, n_sub, part, 0)
        return 0

    lax.fori_loop(1, zs + 1, step, 0)
    over_shards(zs - 1, backward)

    for b in range(nl):
        hg_all[tn * nl + b] = hg_acc[b * HEAD : (b + 1) * HEAD, :].T.astype(BF16)
    hg_copy(tn).start()

    def piece_copy(src, dst, send, recv, to):
        return pltpu.make_async_remote_copy(
            src_ref=src, dst_ref=dst, send_sem=send, recv_sem=recv, device_id=to, device_id_type=MESH
        )

    class Stream:
        def __init__(self, refs, full):
            (self.g, self.from_core, self.from_dp, self.from_z) = refs[:4]
            (self.c_s, self.c_r, self.y_s, self.y_r, self.z_s, self.z_r) = refs[4:10]
            (self.a_r, self.az_s, self.ay_s) = refs[10:13]
            self.full = full
            self.u = self.from_z.shape[1]

        def rows(self, c, e, q):
            return pl.ds(pl.multiple_of(((c * dps + e) * zs + q) * self.u, self.u), self.u)

        def core_copy(self, e, q):
            return piece_copy(
                self.g.at[self.rows(1 - core, e, q)],
                self.from_core.at[e * zs + q],
                self.c_s.at[e, q],
                self.c_r.at[e, q],
                other_core,
            )

        def dp_copy(self, src, e, q):
            return piece_copy(
                self.g.at[self.rows(core, e, q)],
                self.from_dp.at[src * zs + q],
                self.y_s.at[e, q],
                self.y_r.at[src, q],
                {"dp": e},
            )

        def z_copy(self, src, q):
            return piece_copy(
                self.g.at[self.rows(core, dp, q)],
                self.from_z.at[src],
                self.z_s.at[q],
                self.z_r.at[src],
                {"fsdp": 2 * q + core},
            )

        def full_copy(self, c, e, q, send, to):
            piece = self.full.at[self.rows(c, e, q)]
            return piece_copy(piece, piece, send, self.a_r.at[c, e, q], to)

        def gather_z(self, q):
            return self.full_copy(core, dp, z, self.az_s.at[q], {"fsdp": 2 * q + core})

        def gather_dp(self, e, q):
            return self.full_copy(core, dp, q, self.ay_s.at[e, q], {"dp": e})

        def gather_core(self, e, q):
            return self.full_copy(core, e, q, self.c_s.at[e, q], other_core)

        def came(self, c, e, q):
            self.full_copy(c, e, q, self.c_s.at[e, q], other_core).wait_recv()

        def each_q(self, body):
            def one(i, _):
                body((z + 1 + i) % zs)
                return 0

            lax.fori_loop(0, zs, one, 0)

        def each_e(self, body, own=False):
            def one(i, _):
                body((dp + 1 + i) % dps)
                return 0

            lax.fori_loop(0, dps if own else dps - 1, one, 0)

        def start_core(self):
            self.each_e(lambda e: self.each_q(lambda q: self.core_copy(e, q).start()), True)

        def core_sums(self):
            def one(e, q):
                self.core_copy(e, q).wait()
                rows = self.rows(core, e, q)
                total = self.g[rows, :].astype(F32) + self.from_core[e * zs + q].astype(F32)
                self.g[rows, :] = total.astype(BF16)

                @pl.when(e != dp)
                def _():
                    self.dp_copy(dp, e, q).start()

            self.each_e(lambda e: self.each_q(lambda q: one(e, q)), True)

        def dp_sums(self, rows_between, row):
            each = -(-rows_between // zs)

            def one(q):
                for i in range(each):
                    r = q * each + i

                    @pl.when(r < rows_between)
                    def _():
                        row(r)

                rows = self.rows(core, dp, q)
                total = self.g[rows, :].astype(F32)
                for i in range(1, dps):
                    src = (dp + i) % dps
                    self.dp_copy(src, dp, q).wait_recv()
                    total = total + self.from_dp[src * zs + q].astype(F32)
                self.g[rows, :] = total.astype(BF16)

                @pl.when(q != z)
                def _():
                    self.z_copy(z, q).start()

            self.each_q(one)

        def z_sums(self):
            total = self.g[self.rows(core, dp, z), :].astype(F32)
            for i in range(1, zs):
                src = (z + i) % zs
                self.z_copy(src, z).wait_recv()
                total = total + self.from_z[src].astype(F32)
            self.full[self.rows(core, dp, z), :] = total.astype(BF16)

            def to_z(i, _):
                self.gather_z((z + i) % zs).start()
                return 0

            lax.fori_loop(1, zs, to_z, 0)
            self.each_e(lambda e: self.gather_dp(e, z).start())
            self.gather_core(dp, z).start()

        def near(self, body):
            def one(s, _):
                for zz in (z - s, z + s):
                    @pl.when((zz >= 0) & (zz < zs))
                    def _():
                        body(zz)

                return 0

            lax.fori_loop(1, zs, one, 0)

        def forward_z(self):
            def one(q):
                self.came(core, dp, q)
                self.each_e(lambda e: self.gather_dp(e, q).start())
                self.gather_core(dp, q).start()

            self.near(one)

        def forward_dp(self):
            def one(q):
                def each(e):
                    self.came(core, e, q)
                    self.gather_core(e, q).start()

                self.each_e(each)

            one(z)
            self.near(one)

        def finish(self):
            self.each_e(lambda e: self.each_q(lambda q: self.came(1 - core, e, q)), True)

        def drain(self):
            self.each_e(lambda e: self.each_q(lambda q: self.dp_copy(dp, e, q).wait_send()))
            self.each_e(lambda e: self.each_q(lambda q: self.gather_dp(e, q).wait_send()))
            self.each_e(lambda e: self.each_q(lambda q: self.gather_core(e, q).wait_send()), True)

            def to_z(i, _):
                self.z_copy(z, (z + i) % zs).wait_send()
                self.gather_z((z + i) % zs).wait_send()
                return 0

            lax.fori_loop(1, zs, to_z, 0)

        def clear_tail(self, used):
            spare = self.g.shape[0] - used
            if spare > 0:
                self.g[used:, :] = jnp.zeros((spare, HEAD), BF16)

    outs, ins = Stream(streams[0], out_full), Stream(streams[1], in_full)
    outs.clear_tail(pairs_out * HEAD)
    ins.clear_tail(rows_in * k_in * HEAD)

    def add_shard(f, _):
        chunk_copy(p_mine, p_theirs, p_send, p_recv, f).wait_recv()
        for b in range(nb):
            oo[f * nb + b] = (
                p_mine[f * nb + b].astype(F32) + p_theirs[f * nb + b].astype(F32)
            ).astype(BF16)
        return 0

    lax.fori_loop(0, 2 * zs, add_shard, 0)

    def halves(stream, rows, terms, row):
        half = stream.g.shape[0] // (2 * HEAD * terms)
        whole = rows == 2 * half
        unroll = max(n for n in (1, 2, 3, 4, 5) if half % n == 0) if whole else 1

        def run(c):
            def one(i, _):
                r = c * half + i
                if whole:
                    row(r)
                else:
                    pl.when(r < rows)(lambda: row(r))
                return 0

            lax.fori_loop(0, half, one, 0, unroll=unroll)

        run(1 - core)
        stream.start_core()
        run(core)

    def out_row(r):
        cols = pl.ds(pl.multiple_of(r * HEAD, HEAD), HEAD)
        for k in range(k_out):
            to = pl.ds(pl.multiple_of((r * k_out + k) * HEAD, HEAD), HEAD)
            outs.g[to, :] = dot(oo[out_col(r, k)], cot[:, cols], 0, 0).astype(BF16)

    def in_row(r):
        mine = tn * rows_in + r
        mine_cols = pl.ds(pl.multiple_of(mine * HEAD, HEAD), HEAD)
        for k in range(k_in):
            block = hg_all[in_col(mine, k)]
            to = pl.ds(pl.multiple_of((r * k_in + k) * HEAD, HEAD), HEAD)
            ins.g[to, :] = dot(attn[:, mine_cols], block, 0, 0).astype(BF16)

    halves(outs, rows_out, k_out, out_row)
    outs.core_sums()
    hg_copy(1 - tn).wait_recv()
    halves(ins, rows_in, k_in, in_row)
    ins.core_sums()

    def grown_row(r):
        cols = pl.ds(pl.multiple_of(r * HEAD, HEAD), HEAD)
        total = None
        for k in range(k_out):
            term = dot(oo[out_col(r, k)], out_b[r * k_out + k])
            total = term if total is None else total + term
        grown[:, cols] = total.astype(BF16)

    def gattn_row(r):
        cols = pl.ds(pl.multiple_of(r * HEAD, HEAD), HEAD)
        mine = tn * rows_in + r
        total = None
        for k in range(k_in):
            term = dot(hg_all[in_col(mine, k)], in_b[mine * k_in + k], 1, 1)
            total = term if total is None else total + term
        gattn[:, cols] = total.astype(BF16)

    outs.dp_sums(rows_out, grown_row)
    ins.dp_sums(rows_in, gattn_row)
    outs.z_sums()
    ins.z_sums()
    outs.forward_z()
    ins.forward_z()
    outs.forward_dp()
    ins.forward_dp()
    outs.finish()
    ins.finish()
    outs.drain()
    ins.drain()

    def send_done(f, _):
        chunk_copy(og_mine, og_theirs, og_send, og_recv, f).wait_send()
        chunk_copy(p_mine, p_theirs, p_send, p_recv, f).wait_send()
        return 0

    lax.fori_loop(0, 2 * zs, send_done, 0)
    hg_copy(tn).wait_send()

    def own_done(q, _):
        @pl.when(z < zs - 1)
        def _():
            w_copy(fs, h, q, 0, above).wait_send()

        @pl.when(z > 0)
        def _():
            w_copy(fs, h, q, 1, below).wait_send()

        w_copy(fs, h, q, 3, other_core).wait_send()
        w_copy(fs, o, q, 3, other_core).wait_send()
        return 0

    lax.fori_loop(0, n_sub, own_done, 0)

    def relay_done(i, _):
        s = 1 + i // n_sub
        q = i % n_sub
        for way in range(2):
            zz = z - s + 2 * s * way
            nxt = z + 1 - 2 * way
            f = 2 * zz + core

            @pl.when((zz >= 0) & (zz < zs))
            def _():
                @pl.when((nxt >= 0) & (nxt < zs))
                def _():
                    w_copy(f, h, q, way, above if way == 0 else below).wait_send()

                w_copy(f, h, q, 2, other_dp).wait_send()
                w_copy(f, h, q, 3, other_core).wait_send()
                w_copy(f, o, q, 3, other_core).wait_send()

        return 0

    lax.fori_loop(0, (zs - 1) * n_sub, relay_done, 0)


def finish_kernel(
    scale, grown_in, gattn_in, out_in, in_in, grown, gattn, out_sum, in_sum, out_buf, in_buf, sems
):
    copies = [
        pltpu.make_async_copy(grown_in, grown, sems.at[0]),
        pltpu.make_async_copy(gattn_in, gattn, sems.at[1]),
    ]
    for one in copies:
        one.start()
    spot = 2
    for src, buf, dst, parts in ((out_in, out_buf, out_sum, 4), (in_in, in_buf, in_sum, 2)):
        blocks = buf.shape[0]
        for i in range(parts):
            lo, hi = blocks * i // parts, blocks * (i + 1) // parts

            def block(b, _):
                rows = pl.ds(pl.multiple_of(b * HEAD, HEAD), HEAD)
                buf[b] = src[rows, :].astype(F32) * scale
                return 0

            lax.fori_loop(lo, hi, block, 0)
            part = pl.ds(lo, hi - lo)
            copies.append(pltpu.make_async_copy(buf.at[part], dst.at[part], sems.at[spot]))
            copies[-1].start()
            spot += 1
    for one in copies:
        one.wait()


def index_table(pick, in_cols, out_cols, targets):
    pairs = max(in_cols.size, out_cols.size)
    flats, orders = [], []
    for cols in (in_cols, out_cols):
        rows, terms = cols.shape
        short = (0, pairs - cols.size)
        order = jnp.arange(rows, dtype=jnp.int32)[None, :] * terms
        order = order + jnp.arange(terms, dtype=jnp.int32)[:, None]
        flats.append(jnp.pad(cols.T.reshape(-1), short, constant_values=-1))
        orders.append(jnp.pad(order.reshape(-1), short, constant_values=pairs))
    flat, order = jnp.stack(flats), jnp.stack(orders)
    named = jnp.broadcast_to(jnp.arange(targets, dtype=jnp.int32), (2, targets))
    want = jnp.concatenate([flat, named], axis=1)
    limit = jnp.concatenate([order, jnp.full((2, targets), pairs, jnp.int32)], axis=1)
    same = (want[:, :, None] == flat[:, None, :]) & (order[:, None, :] < limit[:, :, None])
    found = jnp.max(jnp.where(same, order[:, None, :], -1), axis=2)
    found = jnp.where(found < 0, pairs, found)
    return jnp.concatenate([pick, flat.reshape(-1), found.reshape(-1)])


def local(
    attn_out,
    cotangent,
    old_weights,
    depth_coef,
    depth_pick,
    in_blocks,
    in_cols,
    out_blocks,
    out_cols,
):
    tok = attn_out.shape[0]
    fsdp = lax.axis_size("fsdp")
    tensor = lax.axis_size("tensor")
    dps = lax.axis_size("dp")
    zs = fsdp // 2
    _, feats, shard = old_weights.shape
    n_out = fsdp * shard // HEAD
    n_in = tensor * feats // HEAD
    rows_all, k_in = in_cols.shape
    rows_out, k_out = out_cols.shape
    rows_in = rows_all // tensor
    pairs_in, pairs_out = rows_all * k_in, rows_out * k_out
    depth_k = depth_pick.shape[0]
    smem = pl.BlockSpec(memory_space=pltpu.SMEM)
    vmem = pl.BlockSpec(memory_space=pltpu.VMEM)
    dma = pltpu.SemaphoreType.DMA
    blocks = (n_out, tok, HEAD)
    scale = float(tok * dps * fsdp) ** (-0.5)

    n_sub = 4
    pairs = max(pairs_in, pairs_out)

    def stream_rows(rows):
        return -(-rows // (2 * dps * zs * 16)) * 16

    def stream_scratch(rows):
        u = stream_rows(rows)
        return [
            pltpu.VMEM((2 * dps * zs * u, HEAD), BF16),
            pltpu.VMEM((dps * zs, u, HEAD), BF16),
            pltpu.VMEM((dps * zs, u, HEAD), BF16),
            pltpu.VMEM((zs, u, HEAD), BF16),
            dma((dps, zs)),
            dma((dps, zs)),
            dma((dps, zs)),
            dma((dps, zs)),
            dma((zs,)),
            dma((zs,)),
            dma((2, dps, zs)),
            dma((zs,)),
            dma((dps, zs)),
        ]

    def stream_out(rows):
        return jax.ShapeDtypeStruct((2 * dps * zs * stream_rows(rows), HEAD), BF16)

    rows_o, rows_i = pairs_out * HEAD, rows_in * k_in * HEAD
    arrays = (
        attn_out,
        cotangent,
        old_weights,
        in_blocks.reshape(pairs_in, HEAD, HEAD),
        out_blocks.reshape(pairs_out, HEAD, HEAD),
    )
    grown, gattn, out_sum, in_sum = pl.pallas_call(
        functools.partial(
            kernel, (zs, dps, depth_k, k_in, k_out, rows_all, rows_out, pairs, n_sub)
        ),
        out_shape=(
            jax.ShapeDtypeStruct((tok, rows_out * HEAD), BF16),
            jax.ShapeDtypeStruct((tok, rows_in * HEAD), BF16),
            stream_out(rows_o),
            stream_out(rows_i),
        ),
        in_specs=[smem] * 2 + [pl.BlockSpec(memory_space=pl.ANY)] * 5,
        out_specs=(vmem, vmem, vmem, vmem),
        scratch_shapes=[
            pltpu.VMEM(attn_out.shape, BF16),
            pltpu.VMEM(cotangent.shape, BF16),
            pltpu.VMEM((old_weights.shape[0], feats // 2, shard), BF16),
            pltpu.VMEM((old_weights.shape[0], feats // 2, shard), BF16),
            pltpu.VMEM(arrays[3].shape, BF16),
            pltpu.VMEM(arrays[4].shape, BF16),
            dma((6,)),
            pltpu.VMEM((fsdp, feats, shard), BF16),
            pltpu.VMEM((pairs + 1, tok, HEAD), F32),
            pltpu.VMEM(blocks, BF16),
            pltpu.VMEM(blocks, BF16),
            pltpu.VMEM(blocks, BF16),
            pltpu.VMEM(blocks, BF16),
            pltpu.VMEM(blocks, BF16),
            pltpu.VMEM((tok, feats), BF16),
            pltpu.VMEM((feats, tok), F32),
            pltpu.VMEM((n_in, tok, HEAD), BF16),
            dma((fsdp, 2, n_sub, 4)),
            dma((fsdp, 2, n_sub)),
            dma((fsdp,)),
            dma((fsdp,)),
            dma((fsdp,)),
            dma((fsdp,)),
            dma,
            dma,
            *stream_scratch(rows_o),
            *stream_scratch(rows_i),
        ],
        compiler_params=pltpu.CompilerParams(
            collective_id=0, has_side_effects=True, vmem_limit_bytes=52 * 2**20
        ),
    )(
        index_table(depth_pick, in_cols, out_cols, max(n_in, n_out)),
        depth_coef,
        *arrays,
    )
    anywhere = pl.BlockSpec(memory_space=pl.ANY)
    out_blocks_shape = (pairs_out, HEAD, HEAD)
    in_blocks_shape = (rows_in * k_in, HEAD, HEAD)
    grown, gattn, out_sum, in_sum = pl.pallas_call(
        functools.partial(finish_kernel, scale),
        out_shape=(
            jax.ShapeDtypeStruct(grown.shape, BF16),
            jax.ShapeDtypeStruct(gattn.shape, BF16),
            jax.ShapeDtypeStruct(out_blocks_shape, F32),
            jax.ShapeDtypeStruct(in_blocks_shape, F32),
        ),
        in_specs=[anywhere, anywhere, vmem, vmem],
        out_specs=(anywhere,) * 4,
        scratch_shapes=[
            pltpu.VMEM(out_blocks_shape, F32),
            pltpu.VMEM(in_blocks_shape, F32),
            dma((8,)),
        ],
        compiler_params=pltpu.CompilerParams(vmem_limit_bytes=16 * 2**20),
    )(grown, gattn, out_sum, in_sum)
    in_sum = in_sum.reshape(rows_in, k_in, HEAD, HEAD)
    out_sum = out_sum.reshape(rows_out, k_out, HEAD, HEAD)
    return grown, gattn, in_sum, out_sum


def solution(mesh):
    placed = (
        P(("dp", "fsdp"), None),
        P(("dp", "fsdp"), "tensor"),
        P(None, "tensor", "fsdp"),
        P(),
        P(),
        P(),
        P(),
        P("tensor", None, None, None),
        P("tensor", None),
    )
    return jax.shard_map(
        local,
        mesh=mesh,
        in_specs=placed,
        out_specs=(
            P(("dp", "fsdp"), "tensor"),
            P(("dp", "fsdp"), "tensor"),
            P("tensor", None, None, None),
            P("tensor", None, None, None),
        ),
        check_vma=False,
    )
```
